128 devices in a mesh: row: 16 (over y, z_lo, core), col: 8 (over z_hi, x).
Axes of the slice: x: 4, y: 4, z: 4 (z_hi: 2, z_lo: 2; z = z_hi * 2 + z_lo), core: 2. Of those that a mesh axis runs over, the one named last changes fastest.
Arguments:
- single: float32 [1024, 768], P('row', 'col'), may hold values from -6 to 6
- pair: float32 [1024, 1024, 128], P('row', 'col'), may hold values from -6 to 6
- single_gain: float32 [768], replicated, may hold values from 0.25 to 1.75
- pair_gain: float32 [128], replicated, may hold values from 0.25 to 1.75
- w_query: float32 [768, 768], replicated, may hold values from -0.25 to 0.25
- w_key: float32 [768, 768], replicated, may hold values from -0.25 to 0.25
- w_value: float32 [768, 768], replicated, may hold values from -0.21875 to 0.21875
- w_gate: float32 [768, 768], replicated, may hold values from -0.21875 to 0.21875
- w_bias: float32 [128, 16], replicated, may hold values from -0.5 to 0.5
- w_out: float32 [768, 768], P(None, 'col'), may hold values from -0.21875 to 0.21875
- cotangent: float32 [1024, 768], P('row', 'col'), may hold values from -6 to 6
Outputs:
- attended: float32 [1024, 768], P('row', 'col')
- pair_grad: float32 [1024, 1024, 128], P('row', 'col')
- bias_grad: float32 [128, 16], replicated
The draws below stay inside these ranges and needn't reach their ends.
All inputs are finite; a program needn't handle non-finite values.
Results may differ from the reference program's by a relative error of at most 0.0003.
Values sent between devices are 32-bit elements; how exact they have to be, the bound alone decides.
No kernel may reach another device: no remote copies, remote signals or barrier semaphores. Data moves between devices by JAX's collectives and lax.ppermute only.
A program may use at most 128 MiB of HBM per device.

```python
import jax
import jax.numpy as jnp
from jax import lax

D = 768
HEADS = 16
PAIR_C = 128
TR = 64
TOKENS = 1024
N_ROW = 16


def projection(key, salt):
    key = jax.random.fold_in(key, salt)
    matrix = jax.random.normal(key, (D, D), jnp.float32) * D ** (-0.5)
    matrix = jnp.clip(matrix, -6.0 * D ** (-0.5), 6.0 * D ** (-0.5))
    return jnp.clip(matrix, -0.25, 0.25)


def draw_single(key, part):
    key = jax.random.fold_in(key, 11)
    base = jax.random.normal(key, (TOKENS, D), jnp.float32)
    return jnp.clip(base, -6.0, 6.0)


def draw_w_query(key, part):
    return projection(key, 23)


def draw_w_key(key, part):
    return projection(key, 37)


def block_scale(key, dims, pieces, smallest, top_value):
    def one(position, blocks):
        heights = jax.random.uniform(jax.random.fold_in(jax.random.fold_in(key, 6), position), (blocks,), jnp.float32, smallest / len(pieces), top_value / len(pieces))
        return jnp.repeat(jnp.exp(heights), dims[position] // blocks).reshape((-1,) + (1,) * (len(dims) - position - 1))

    loudness = one(*pieces[0])
    for cut in pieces[1:]:
        loudness = loudness * one(*cut)
    return loudness


def scatter_about(stream_key, shape, scale, reach, pieces=(), held_as=jnp.bfloat16):
    level = block_scale(stream_key, shape, pieces, -0.22, 0.18) if pieces else 1.0
    drawn = jax.random.normal(stream_key, shape, jnp.float32) * scale * level
    return jnp.minimum(jnp.maximum(drawn, -reach), reach).astype(held_as)


def setup_inputs(seed: int = 0) -> dict:
    seeds = jax.random.split(jax.random.key(seed), 12)
    single = draw_single(jax.random.fold_in(seeds[11], 71), 0)
    pair = scatter_about(seeds[1], (TOKENS, TOKENS, PAIR_C), 1.0, 6.0, ((0, 16), (1, 8)), jnp.float32)
    single_gain = jnp.clip(1.0 + 0.15 * jax.random.normal(seeds[2], (D,), jnp.float32), 0.25, 1.75)
    pair_gain = jnp.clip(1.0 + 0.15 * jax.random.normal(seeds[3], (PAIR_C,), jnp.float32), 0.25, 1.75)
    w_query = draw_w_query(jax.random.fold_in(seeds[11], 71), 0)
    w_key = draw_w_key(jax.random.fold_in(seeds[11], 71), 0)
    w_value = scatter_about(seeds[6], (D, D), D ** -0.5, 0.21875, (), jnp.float32)
    w_gate = scatter_about(seeds[7], (D, D), D ** -0.5, 0.21875, (), jnp.float32)
    w_bias = scatter_about(seeds[8], (PAIR_C, HEADS), PAIR_C ** -0.5, 0.5, (), jnp.float32)
    w_out = scatter_about(seeds[9], (D, D), D ** -0.5, 0.21875, ((1, 8),), jnp.float32)
    cotangent = scatter_about(seeds[10], (TOKENS, D), 1.0, 6.0, ((0, 16), (1, 8)), jnp.float32)
    return dict(single=single, pair=pair, single_gain=single_gain, pair_gain=pair_gain, w_query=w_query, w_key=w_key, w_value=w_value, w_gate=w_gate, w_bias=w_bias, w_out=w_out, cotangent=cotangent)


def layer_norm(values_in, gain):
    centre = lax.optimization_barrier(jnp.mean(values_in, axis=-1, keepdims=True))
    spread = lax.optimization_barrier(jnp.mean((values_in - centre) ** 2, axis=-1, keepdims=True))
    return (values_in - centre) * lax.rsqrt(spread + 1e-05) * gain

def reference(single, pair, single_gain, pair_gain, w_query, w_key, w_value, w_gate, w_bias, w_out, cotangent):
    highest = lax.Precision.HIGHEST
    head_dim = D // HEADS
    normed = layer_norm(single, single_gain)
    query = jnp.dot(normed, w_query, precision=highest).reshape(TOKENS, HEADS, head_dim)
    keys = jnp.dot(normed, w_key, precision=highest).reshape(TOKENS, HEADS, head_dim)
    values = jnp.dot(normed, w_value, precision=highest).reshape(TOKENS, HEADS, head_dim)
    gating = jax.nn.sigmoid(jnp.dot(normed, w_gate, precision=highest))
    scale = head_dim ** (-0.5)

    def bias_of(pair_rows, weight):
        return jnp.einsum('ijc,ch->ihj', layer_norm(pair_rows, pair_gain), weight, precision=highest)

    def weights_of(index):
        start = (index * TR).astype(jnp.int32)
        query_rows = lax.dynamic_slice_in_dim(query, start, TR, 0)
        pair_rows = lax.dynamic_slice_in_dim(pair, start, TR, 0)
        scores = jnp.einsum('ihd,jhd->ihj', query_rows, keys, precision=highest) * scale + bias_of(pair_rows, w_bias)
        return (jax.nn.softmax(scores, axis=-1), pair_rows)

    def forward_block(index):
        soft_weights, _ = weights_of(index)
        return jnp.einsum('ihj,jhd->ihd', soft_weights, values, precision=highest)
    blocks = jnp.arange(N_ROW, dtype=jnp.int32)
    context = lax.map(forward_block, blocks).reshape(TOKENS, D)
    attended = jnp.dot(gating * context, w_out, precision=highest)
    d_context = (jnp.dot(cotangent, w_out.T, precision=highest) * gating).reshape(TOKENS, HEADS, head_dim)
    row_delta_all = lax.optimization_barrier(jnp.sum(d_context * context.reshape(TOKENS, HEADS, head_dim), axis=-1))

    def backward_block(index):
        soft_weights, pair_rows = weights_of(index)
        start = (index * TR).astype(jnp.int32)
        d_rows = lax.dynamic_slice_in_dim(d_context, start, TR, 0)
        row_delta = lax.dynamic_slice_in_dim(row_delta_all, start, TR, 0)
        d_probs = jnp.einsum('ihd,jhd->ihj', d_rows, values, precision=highest)
        d_scores = soft_weights * (d_probs - row_delta[:, :, None])
        _, pull = jax.vjp(bias_of, pair_rows, w_bias)
        return pull(d_scores)
    pair_parts, weight_parts = lax.map(backward_block, blocks)
    pair_grad = pair_parts.reshape(TOKENS, TOKENS, PAIR_C)
    bias_grad = lax.optimization_barrier(jnp.sum(weight_parts, axis=0))
    return (attended, pair_grad, bias_grad)
```

```python
import functools

import jax
import jax.numpy as jnp
from jax import lax
from jax.experimental import pallas as pl
from jax.experimental.pallas import tpu as pltpu
from jax.sharding import PartitionSpec as P

F32 = jnp.float32
BF16 = jnp.bfloat16
EPS = 1e-05
NN = (((1,), (0,)), ((), ()))
NT = (((1,), (1,)), ((), ()))
TN = (((0,), (0,)), ((), ()))
VMEM_LIMIT = 48 * 1024 * 1024


def split(x):
    high = x.astype(BF16)
    return high, (x - high.astype(F32)).astype(BF16)


def dg(a, b, dims):
    return lax.dot_general(a, b, dims, preferred_element_type=F32)


def dot3(a, b, dims):
    ah, al = split(a)
    bh, bl = split(b)
    return dg(ah, bh, dims) + dg(al, bh, dims) + dg(ah, bl, dims)


def call(kernel, out_shape, flops, args, grid=None, in_specs=None, out_specs=None, scratch=()):
    nbytes = sum(a.size * a.dtype.itemsize for a in args)
    for o in jax.tree.leaves(out_shape):
        nbytes += o.size * jnp.dtype(o.dtype).itemsize
    kw = {}
    if grid is not None:
        kw = dict(grid=grid, in_specs=in_specs, out_specs=out_specs)
    return pl.pallas_call(
        kernel,
        out_shape=out_shape,
        scratch_shapes=list(scratch),
        compiler_params=pltpu.CompilerParams(vmem_limit_bytes=VMEM_LIMIT),
        cost_estimate=pl.CostEstimate(flops=flops, bytes_accessed=nbytes, transcendentals=0),
        **kw,
    )(*args)


def sds(*shape, dtype=F32):
    return jax.ShapeDtypeStruct(shape, dtype)


def head_mask(heads, width):
    lane = lax.broadcasted_iota(jnp.int32, (heads, width), 1)
    row = lax.broadcasted_iota(jnp.int32, (heads, width), 0)
    size = width // heads
    return (lane >= row * size) & (lane < (row + 1) * size)


def eye_mask(n):
    return lax.broadcasted_iota(jnp.int32, (n, n), 0) == lax.broadcasted_iota(jnp.int32, (n, n), 1)


def first_kernel(single_ref, cot_ref, wout_ref, out_ref):
    n, _, block = out_ref.shape
    rows = single_ref.shape[0]
    single = single_ref[...]
    cot = cot_ref[...]
    for k in range(n):
        out_ref[k, :rows] = single
        out_ref[k, rows:] = dot3(cot, wout_ref[k * block : (k + 1) * block, :], NT)


def back_kernel(recv_ref, out_ref):
    n, rows, _ = out_ref.shape
    total = recv_ref[0, rows:]
    for k in range(1, n):
        total = total + recv_ref[k, rows:]
    for k in range(n):
        out_ref[k] = total


def joined_norm(blocks, gain_ref, out_ref, row):
    rows, block = blocks[0].shape
    width = block * len(blocks)
    centre = sum(jnp.sum(b, axis=-1, keepdims=True) for b in blocks) / width
    blocks = [b - centre for b in blocks]
    spread = sum(jnp.sum(b * b, axis=-1, keepdims=True) for b in blocks) / width
    scale = lax.rsqrt(spread + EPS)
    for k, b in enumerate(blocks):
        part = slice(k * block, (k + 1) * block)
        out_ref[row : row + rows, part] = b * scale * gain_ref[:, part]


def query_kernel(recv_ref, gain_ref, wq_ref, wg_ref, query_ref, gate_ref, normed):
    n = recv_ref.shape[0]
    rows = query_ref.shape[0]
    joined_norm([recv_ref[k, :rows] for k in range(n)], gain_ref, normed, 0)
    query_ref[...] = dot3(normed[...], wq_ref[...], NN) * (48 ** -0.5)
    logits = dot3(normed[...], wg_ref[...], NN)
    gate_ref[...] = 1.0 / (1.0 + jnp.exp(-logits))


def pair_kernel(pair_ref, wt_ref, high_ref, low_ref, bias_ref, rs_ref):
    steps, keys, chans = pair_ref.shape
    heads = bias_ref.shape[1]
    wh, wl = split(wt_ref[...])
    both = jnp.concatenate([wh, wl], axis=0)
    ones = jnp.ones((8, chans), BF16)
    for i in range(steps):
        x = pair_ref[i]
        d = x - jnp.sum(x, axis=-1, keepdims=True) * (1.0 / chans)
        dh, dl = split(d)
        high_ref[i] = dh
        low_ref[i] = dl
        sh, sl = split(d * d)
        spread = (dg(ones, sh, NT) + dg(ones, sl, NT)) * (1.0 / chans)
        rs = lax.rsqrt(spread + EPS)
        two = dg(both, dh, NT)
        raw = two[:heads] + two[heads:] + dg(wh, dl, NT)
        bias_ref[i] = raw * rs[0:1]
        rs_ref[i : i + 1, :] = rs[0:1]


def attend_kernel(
    recv_ref, back_ref, gain_ref, wk_ref, wv_ref, query_ref, gate_ref, bias_ref,
    pay_ref, expo_ref, dprobs_ref, max_ref,
    normed, dctx, acc,
):
    n_row, rows, block = recv_ref.shape
    n_col = back_ref.shape[0]
    queries, heads, keys = bias_ref.shape
    width = normed.shape[1]
    per = n_row // n_col
    for t in range(per):
        joined_norm(
            [recv_ref[t * n_col + k] for k in range(n_col)], gain_ref, normed, t * rows
        )
    kh, kl = split(dot3(normed[...], wk_ref[...], NN))
    vh, vl = split(dot3(normed[...], wv_ref[...], NN))
    for k in range(n_col):
        part = slice(k * block, (k + 1) * block)
        dctx[:, part] = back_ref[k] * gate_ref[:, part]
    mask = head_mask(heads, width)[None]
    eye = eye_mask(heads)[None]
    chunk = 16
    size = chunk * heads

    def step(s, carry):
        here = pl.ds(pl.multiple_of(s * chunk, chunk), chunk)

        def spread(rows_):
            wide = jnp.where(mask, rows_[:, None, :], 0.0)
            h, l = split(wide)
            return h.reshape(size, width), l.reshape(size, width)

        qh, ql = spread(query_ref[here])
        scores = dg(qh, kh, NT) + dg(ql, kh, NT) + dg(qh, kl, NT)
        scores = scores + bias_ref[here].reshape(size, keys)
        gh, gl = spread(dctx[here])
        dp = dg(gh, vh, NT) + dg(gl, vh, NT) + dg(gh, vl, NT)
        top = jnp.max(scores, axis=-1, keepdims=True)
        expo = jnp.exp(scores - top)
        total = jnp.sum(expo, axis=-1, keepdims=True)
        inv = 1.0 / total
        delta = jnp.sum(expo * dp, axis=-1, keepdims=True) * inv
        expo_ref[here] = expo.reshape(chunk, heads, keys)
        dprobs_ref[here] = dp.reshape(chunk, heads, keys)
        eh, el = split(expo * inv)
        wide = dg(eh, vh, NN) + dg(el, vh, NN) + dg(eh, vl, NN)
        acc[here] = jnp.sum(jnp.where(mask, wide.reshape(chunk, heads, width), 0.0), axis=1)

        def lanes(col):
            return jnp.sum(jnp.where(eye, col.reshape(chunk, heads, 1), 0.0), axis=1)

        lse = lanes(top + jnp.log(total))
        dlt = lanes(delta)
        max_ref[here] = lanes(top)
        for k in range(n_col):
            pay_ref[k, here, block : block + heads] = lse
            pay_ref[k, here, block + heads : block + 2 * heads] = dlt
        return carry

    lax.fori_loop(0, queries // chunk, step, 0)
    for k in range(n_col):
        pay_ref[k, :, :block] = acc[:, k * block : (k + 1) * block]


def moment_kernel(high_ref, low_ref, expo_ref, dprobs_ref, rs_ref, out_ref):
    steps, heads, keys = expo_ref.shape
    for i in range(steps):
        e = expo_ref[i] * rs_ref[i : i + 1, :]
        both = jnp.concatenate([e * dprobs_ref[i], e], axis=0)
        bh, bl = split(both)
        dh = high_ref[i]
        first = dg(jnp.concatenate([bh, bl], axis=0), dh, NN)
        out_ref[i] = first[: 2 * heads] + first[2 * heads :] + dg(bh, low_ref[i], NN)


def join_kernel(recv_ref, max_ref, moment_ref, pgain_ref, sel_ref, pay_ref, fac_ref, dlt_ref):
    n, rows, _ = recv_ref.shape
    heads = max_ref.shape[1]
    block = sel_ref.shape[1]
    lse = [recv_ref[k, :, block : block + heads] for k in range(n)]
    top = functools.reduce(jnp.maximum, lse)
    weight = [jnp.exp(v - top) for v in lse]
    total = sum(weight)
    inv = 1.0 / total
    weight = [w * inv for w in weight]
    delta = sum(w * recv_ref[k, :, block + heads :] for k, w in enumerate(weight))
    fac = jnp.exp(max_ref[...] - (top + jnp.log(total)))
    fac_ref[...] = fac
    dlt_ref[...] = delta
    sel = sel_ref[...]
    context = sum(
        lax.dot_general(w, sel, NN, precision=lax.Precision.HIGHEST, preferred_element_type=F32)
        * recv_ref[k, :, :block]
        for k, w in enumerate(weight)
    )
    eye = eye_mask(heads)[None]

    def column(v):
        return jnp.sum(jnp.where(eye, v[:, None, :], 0.0), axis=-1, keepdims=True)

    part = jnp.sum(
        column(fac) * moment_ref[:, :heads] - column(fac * delta) * moment_ref[:, heads:], axis=0
    ) * pgain_ref[...]
    for k in range(n):
        pay_ref[k, :rows, :block] = context
        pay_ref[k, rows:, :] = part


def grad_kernel(high_ref, low_ref, expo_ref, dprobs_ref, bias_ref, rs_ref, fac_ref, dlt_ref, w_ref, out_ref):
    steps, heads, keys = expo_ref.shape
    chans = out_ref.shape[2]
    eye = eye_mask(heads)
    wh, wl = split(w_ref[...])
    weights = jnp.concatenate([wh, wh, wl], axis=0)
    for i in range(steps):
        fac = jnp.sum(jnp.where(eye, fac_ref[i : i + 1, :], 0.0), axis=-1, keepdims=True)
        dlt = jnp.sum(jnp.where(eye, dlt_ref[i : i + 1, :], 0.0), axis=-1, keepdims=True)
        rs = rs_ref[i : i + 1, :]
        u = expo_ref[i] * fac * (dprobs_ref[i] - dlt) * rs
        both = jnp.concatenate([u, u * bias_ref[i] * rs], axis=0)
        bh, bl = split(both)
        wide = dg(jnp.concatenate([bh, bl, bh], axis=0), weights, TN)
        d = high_ref[i].astype(F32) + low_ref[i].astype(F32)
        out_ref[i] = wide[:, :chans] - d * wide[:, chans:]


def out_kernel(recv_ref, gate_ref, wout_ref, att_ref, pay_ref, gated):
    n, _, _ = recv_ref.shape
    rows, block = att_ref.shape
    for k in range(n):
        part = slice(k * block, (k + 1) * block)
        gated[:, part] = recv_ref[k, :rows, :block] * gate_ref[:, part]
    att_ref[...] = dot3(gated[...], wout_ref[...], NN)
    total = recv_ref[0, rows:, :]
    for k in range(1, n):
        total = total + recv_ref[k, rows:, :]
    for k in range(pay_ref.shape[0]):
        pay_ref[k] = total


def last_kernel(recv_ref, out_ref):
    total = recv_ref[0]
    for k in range(1, recv_ref.shape[0]):
        total = total + recv_ref[k]
    out_ref[...] = total.T


def swap(x, axis):
    return lax.all_to_all(x, axis, 0, 0, tiled=True)


def local(
    single, pair, single_gain, pair_gain, w_query, w_key, w_value, w_gate, w_bias, w_out, cotangent
):
    n_row, n_col = lax.axis_size("row"), lax.axis_size("col")
    queries, keys, chans = pair.shape
    heads = w_bias.shape[1]
    width = single_gain.shape[0]
    block = single.shape[1]
    per = n_row // n_col
    gain = single_gain[None]
    pgain = pair_gain[None]

    pay = call(first_kernel, sds(n_col, 2 * queries, block), 2 * queries * width * block * 3, (single, cotangent, w_out))
    perm = [
        (r * n_col + c, ((r % per) * n_col + c) * n_col + r // per)
        for r in range(n_row)
        for c in range(n_col)
    ]
    moved = lax.ppermute(single, ("row", "col"), perm)
    recv1 = swap(pay, "col")
    recv2 = swap(jnp.broadcast_to(moved[None], (n_row,) + moved.shape), "row")

    wt = (pair_gain[:, None] * w_bias).T
    ib = 8
    grid = (queries // ib,)

    def cut(*shape):
        zeros = (0,) * (len(shape))
        return pl.BlockSpec((ib,) + shape, lambda i: (i,) + zeros)

    def whole(a):
        zeros = (0,) * a.ndim
        return pl.BlockSpec(a.shape, lambda i: zeros)

    high, low, bias, rs = call(
        pair_kernel,
        (
            sds(queries, keys, chans, dtype=BF16),
            sds(queries, keys, chans, dtype=BF16),
            sds(queries, heads, keys),
            sds(queries, keys),
        ),
        queries * keys * chans * 400,
        (pair, wt),
        grid,
        [cut(keys, chans), whole(wt)],
        (cut(keys, chans), cut(keys, chans), cut(heads, keys), cut(keys)),
    )
    back_pay = call(back_kernel, sds(n_col, queries, block), queries * width, (recv1,))
    back = swap(back_pay, "col")
    query, gate = call(
        query_kernel,
        (sds(queries, width), sds(queries, width)),
        queries * width * width * 12,
        (recv1, gain, w_query, w_gate),
        scratch=[pltpu.VMEM((queries, width), F32)],
    )
    pay4, expo, dprobs, top = call(
        attend_kernel,
        (
            sds(n_col, queries, block + 2 * heads),
            sds(queries, heads, keys),
            sds(queries, heads, keys),
            sds(queries, heads),
        ),
        keys * width * width * 12,
        (recv2, back, gain, w_key, w_value, query, gate, bias),
        scratch=[
            pltpu.VMEM((keys, width), F32),
            pltpu.VMEM((queries, width), F32),
            pltpu.VMEM((queries, width), F32),
        ],
    )
    recv4 = swap(pay4, "col")
    moment = call(
        moment_kernel,
        sds(queries, 2 * heads, chans),
        queries * keys * chans * heads * 12,
        (high, low, expo, dprobs, rs),
        grid,
        [cut(keys, chans), cut(keys, chans), cut(heads, keys), cut(heads, keys), cut(keys)],
        cut(2 * heads, chans),
    )
    lane = lax.broadcasted_iota(jnp.int32, (heads, block), 1)
    row = lax.broadcasted_iota(jnp.int32, (heads, block), 0)
    size = width // heads
    sel = (row == lax.axis_index("col") * (block // size) + lane // size).astype(F32)
    pay5, fac, dlt = call(
        join_kernel,
        (sds(n_col, queries + heads, chans), sds(queries, heads), sds(queries, heads)),
        queries * heads * chans * 8,
        (recv4, top, moment, pgain, sel),
    )
    recv5 = swap(pay5, "col")
    centred = wt - jnp.mean(wt, axis=1, keepdims=True)
    zero = jnp.zeros_like(centred)
    weights = jnp.concatenate(
        [
            jnp.concatenate([centred, zero], axis=1),
            jnp.concatenate([zero, jnp.full_like(centred, 1.0 / chans)], axis=1),
        ],
        axis=0,
    )
    pair_grad = call(
        grad_kernel,
        sds(queries, keys, chans),
        queries * keys * chans * 400,
        (high, low, expo, dprobs, bias, rs, fac, dlt, weights),
        grid,
        [
            cut(keys, chans), cut(keys, chans), cut(heads, keys), cut(heads, keys), cut(heads, keys),
            cut(keys), cut(heads), cut(heads), whole(weights),
        ],
        cut(keys, chans),
    )
    attended, pay6 = call(
        out_kernel,
        (sds(queries, block), sds(n_row, heads, chans)),
        queries * width * block * 6,
        (recv5, gate, w_out),
        scratch=[pltpu.VMEM((queries, width), F32)],
    )
    recv6 = swap(pay6, "row")
    bias_grad = call(last_kernel, sds(chans, heads), chans * heads, (recv6,))
    return attended, pair_grad, bias_grad


def solution(mesh):
    placed = (
        P("row", "col"),
        P("row", "col", None),
        P(),
        P(),
        P(),
        P(),
        P(),
        P(),
        P(),
        P(None, "col"),
        P("row", "col"),
    )
    return jax.shard_map(
        local,
        mesh=mesh,
        in_specs=placed,
        out_specs=(P("row", "col"), P("row", "col", None), P()),
        check_vma=False,
    )
```

```python
import functools

import jax
import jax.numpy as jnp
from jax import lax
from jax.experimental import pallas as pl
from jax.experimental.pallas import tpu as pltpu
from jax.sharding import PartitionSpec as P

F32 = jnp.float32
BF16 = jnp.bfloat16
EPS = 1e-05
NN = (((1,), (0,)), ((), ()))
NT = (((1,), (1,)), ((), ()))
TN = (((0,), (0,)), ((), ()))
MIB = 1024 * 1024
VMEM_BYTES = 60 * MIB
PARTS = 4
GROUP = 4
FAR = pl.BlockSpec(memory_space=pl.ANY)
NEAR = pl.BlockSpec(memory_space=pltpu.VMEM)


def split(x):
    high = x.astype(BF16)
    return high, (x - high.astype(F32)).astype(BF16)


def dg(a, b, dims):
    return lax.dot_general(a, b, dims, preferred_element_type=F32)


def dot3(a, b, dims):
    ah, al = split(a)
    bh, bl = split(b)
    return dg(ah, bh, dims) + dg(al, bh, dims) + dg(ah, bl, dims)


class Near:
    def __init__(self, src, dst, sem):
        self.copy = pltpu.make_async_copy(src, dst, sem)
        self.copy.start()
        self.dst = dst
        self.waiting = True

    def ready(self):
        if self.waiting:
            self.copy.wait()
            self.waiting = False
        return self.dst


def call(kernel, out_shape, flops, args, scratch=(), near=None, far_out=None, alias=None, vmem=VMEM_BYTES):
    nbytes = sum(a.size * a.dtype.itemsize for a in args)
    for o in jax.tree.leaves(out_shape):
        nbytes += o.size * jnp.dtype(o.dtype).itemsize
    kw = {} if alias is None else {"input_output_aliases": alias}
    scratch = list(scratch)
    body = kernel
    if near is not None:
        kw["in_specs"] = [FAR] * len(args)
        small = [k for k, yes in enumerate(near) if yes]
        scratch += [pltpu.VMEM(args[k].shape, args[k].dtype) for k in small]
        scratch.append(pltpu.SemaphoreType.DMA((len(small),)))

        def body(*refs):
            refs = list(refs)
            places = refs[-len(small) - 1 : -1]
            for n, (k, place_) in enumerate(zip(small, places)):
                refs[k] = Near(refs[k], place_, refs[-1].at[n])
            kernel(*refs[: -len(small) - 1])

    if far_out is not None:
        specs = tuple(FAR if far else NEAR for far in far_out)
        kw["out_specs"] = specs if isinstance(out_shape, tuple) else specs[0]
    return pl.pallas_call(
        body,
        out_shape=out_shape,
        scratch_shapes=scratch,
        compiler_params=pltpu.CompilerParams(vmem_limit_bytes=vmem),
        cost_estimate=pl.CostEstimate(flops=flops, bytes_accessed=nbytes, transcendentals=0),
        **kw,
    )(*args)


class Stream:
    def __init__(self, src, dst, sems, parts=PARTS, shift=0):
        self.src, self.dst, self.sems, self.parts = src, dst, sems, parts
        self.rows = min(src.shape[0], dst.shape[0]) // parts
        self.src_shift = shift if src.shape[0] > dst.shape[0] else 0
        self.dst_shift = shift if src.shape[0] < dst.shape[0] else 0

    def copy(self, k):
        first = pl.multiple_of(k * self.rows, self.rows)
        there = pl.ds(first + self.src_shift, self.rows)
        here = pl.ds(first + self.dst_shift, self.rows)
        return pltpu.make_async_copy(self.src.at[there], self.dst.at[here], self.sems.at[k])

    def start(self):
        for k in range(self.parts):
            self.copy(k).start()

    def wait(self):
        for k in range(self.parts):
            self.copy(k).wait()


def sds(*shape, dtype=F32):
    return jax.ShapeDtypeStruct(shape, dtype)


def head_mask(heads, width):
    lane = lax.broadcasted_iota(jnp.int32, (heads, width), 1)
    row = lax.broadcasted_iota(jnp.int32, (heads, width), 0)
    size = width // heads
    return (lane >= row * size) & (lane < (row + 1) * size)


def eye_mask(n):
    return lax.broadcasted_iota(jnp.int32, (n, n), 0) == lax.broadcasted_iota(jnp.int32, (n, n), 1)


def first_kernel(single_ref, cot_ref, wout_ref, out_ref):
    n, _, lanes = out_ref.shape
    rows, block = single_ref.shape
    rest = lanes - block
    half = rows // 2
    single = single_ref[...]
    ch, cl = split(cot_ref[...])
    wh, wl = split(wout_ref[...])
    two = dg(jnp.concatenate([ch, cl], axis=0), wh, NN)
    full = two[:rows] + two[rows:] + dg(ch, wl, NN)
    for k in range(n):
        part = full[:, k * block : (k + 1) * block]
        out_ref[k, :rows, :block] = single
        out_ref[k, :rows, block:] = part[:, :rest]
        out_ref[k, rows:, : block - rest] = part[:half, rest:]
        out_ref[k, rows:, block - rest :] = part[half:, rest:]


def joined_norm(blocks, out_ref, row):
    rows, block = blocks[0].shape
    width = block * len(blocks)
    centre = sum(jnp.sum(b, axis=-1, keepdims=True) for b in blocks) / width
    blocks = [b - centre for b in blocks]
    spread = sum(jnp.sum(b * b, axis=-1, keepdims=True) for b in blocks) / width
    scale = lax.rsqrt(spread + EPS)
    for k, b in enumerate(blocks):
        part = slice(k * block, (k + 1) * block)
        out_ref[row : row + rows, part] = b * scale


def gained(normed, gain_ref):
    tiles, lanes = gain_ref.shape
    parts = [
        split(normed[:, t * lanes : (t + 1) * lanes] * gain_ref[t : t + 1, :]) for t in range(tiles)
    ]
    return jnp.concatenate(
        [jnp.concatenate([p[k] for p in parts], axis=1) for k in range(2)], axis=0
    )


def project(both, weight, copies):
    rows = both.shape[0] // 2
    third = weight.shape[0] // 3
    out = None
    for k, one in enumerate(copies):
        one.wait()
        here = slice(k * third, (k + 1) * third)
        wh, wl = split(weight[here, :])
        two = dg(both[:, here], wh, NN)
        part = two[:rows] + two[rows:] + dg(both[:rows, here], wl, NN)
        out = part if out is None else out + part
    return out


def fetch(src, dst, sems):
    rows = src.shape[0] // 3
    out = []
    for k in range(3):
        here = pl.ds(k * rows, rows)
        one = pltpu.make_async_copy(src.at[here], dst.at[here], sems.at[k])
        one.start()
        out.append(one)
    return out


def query_kernel(
    pair_far, wb, pgain, recv, gain, wq_far, wg_far,
    bias_far, rs_far, back_ref, query_ref, gate_ref,
    x_ref, bias_ref, rs_ref, sems, normed, wq, wg, qsem, gsem,
):
    take, give = bias_streams(pair_far, bias_far, rs_far, x_ref, bias_ref, rs_ref, sems, 1)
    query_copies = fetch(wq_far, wq, qsem)
    gate_copies = fetch(wg_far, wg, gsem)
    n, rows, block = back_ref.shape
    recv_ref = recv.ready()
    total = recv_ref[0]
    for k in range(1, n):
        total = total + recv_ref[k]
    rest = total.shape[1] - block
    right = jnp.concatenate([total[rows:, : block - rest], total[rows:, block - rest :]], axis=0)
    total = jnp.concatenate([total[:rows, block:], right], axis=1)
    for k in range(n):
        back_ref[k] = total
    bias_rows(take, give, wb.ready(), pgain.ready(), x_ref, bias_ref, rs_ref)
    joined_norm([recv_ref[k, :rows, :block] for k in range(n)], normed, 0)
    both = gained(normed, gain.ready())
    query_ref[...] = project(both, wq, query_copies) * (48 ** -0.5)
    gate_ref[...] = 1.0 / (1.0 + jnp.exp(-project(both, wg, gate_copies)))
    for g in give:
        g.wait()


def centred(x):
    return x - jnp.sum(x, axis=-1, keepdims=True) * (1.0 / x.shape[-1])


def bias_streams(pair_far, bias_far, rs_far, x_ref, bias_ref, rs_ref, sems, part):
    parts = PARTS // 2
    take = Stream(pair_far, x_ref, sems.at[0], parts, part * x_ref.shape[0])
    take.start()
    return take, [Stream(bias_ref, bias_far, sems.at[1], 1), Stream(rs_ref, rs_far, sems.at[2], 1)]


def bias_rows(take, give, wb_ref, pgain_ref, x_ref, bias_ref, rs_ref):
    chans = x_ref.shape[2]
    heads = bias_ref.shape[1]
    wh, wl = split(wb_ref[...] * pgain_ref[...])
    top = jnp.concatenate([wh, wh], axis=1)
    left = jnp.concatenate([top, jnp.concatenate([wl, jnp.zeros_like(wl)], axis=1)], axis=0)
    ones = jnp.ones((8, 2 * chans), BF16)

    def step(k, carry):
        take.copy(k).wait()
        for j in range(take.rows):
            i = k * take.rows + j
            d = centred(x_ref[i])
            spread = dg(ones, jnp.concatenate(split(d * d), axis=1), NT) * (1.0 / chans)
            rs = lax.rsqrt(spread[0:1] + EPS)
            two = dg(left, jnp.concatenate(split(d), axis=1), NT)
            bias_ref[i] = (two[:heads] + two[heads:]) * rs
            rs_ref[pl.ds(i, 1), :] = rs
        return carry

    lax.fori_loop(0, take.parts, step, 0)
    for g in give:
        g.start()


def pair_kernel(pair_far, wb, pgain, bias_far, rs_far, x_ref, bias_ref, rs_ref, sems):
    take, give = bias_streams(pair_far, bias_far, rs_far, x_ref, bias_ref, rs_ref, sems, 0)
    bias_rows(take, give, wb.ready(), pgain.ready(), x_ref, bias_ref, rs_ref)
    for g in give:
        g.wait()


def halves(heads, width):
    return [
        (slice(g * heads // 2, (g + 1) * heads // 2), slice(g * width // 2, (g + 1) * width // 2))
        for g in range(2)
    ]


def by_head(rows, mask):
    wide = jnp.where(mask, rows[:, None, :], 0.0)
    return split(wide.reshape(-1, rows.shape[1]))


def against(rows, mask, high, low):
    keys = high.shape[0]
    rh, rl = by_head(rows, mask)
    two = dg(rh, jnp.concatenate([high, low], axis=0), NT)
    return two[:, :keys] + two[:, keys:] + dg(rl, high, NT)


def score_kernel(
    recv, gain, wk_far, wv_far, query, bias_a, bias_b,
    high_ref, low_ref, expo_ref, acc_ref, stat_ref,
    normed, wk, wv, ksem, vsem,
):
    key_copies = fetch(wk_far, wk, ksem)
    value_copies = fetch(wv_far, wv, vsem)
    recv_ref = recv.ready()
    n_row, rows, block = recv_ref.shape
    queries, heads, keys = expo_ref.shape
    width = normed.shape[1]
    n_col = width // block
    col = lax.axis_index("col")
    for t in range(n_row // n_col):
        joined_norm([recv_ref[place(k, col, t)] for k in range(n_col)], normed, t * rows)
    both = gained(normed, gain.ready())
    kh, kl = split(project(both, wk, key_copies))
    half = heads // 2
    mask = head_mask(half, width // 2)[None]
    eye = eye_mask(half)[None]

    def lanes(column):
        return jnp.sum(jnp.where(eye, column.reshape(queries, half, 1), 0.0), axis=1)

    parts = []
    query_ref = query.ready()
    bias_refs = [bias_a.ready(), bias_b.ready()]
    for some, part in halves(heads, width):
        bias = jnp.concatenate([b[:, some] for b in bias_refs], axis=0)
        scores = against(query_ref[:, part], mask, kh[:, part], kl[:, part])
        scores = scores + bias.reshape(queries * half, keys)
        top = jnp.max(scores, axis=-1, keepdims=True)
        expo = jnp.exp(scores - top)
        total = jnp.sum(expo, axis=-1, keepdims=True)
        inv = 1.0 / total
        expo_ref[:, some] = expo.reshape(queries, half, keys)
        for place_, column in enumerate((top + jnp.log(total), top, inv)):
            first = place_ * heads + some.start
            stat_ref[:, first : first + half] = lanes(column)
        parts.append(split(expo * inv))
    vh, vl = split(project(both, wv, value_copies))
    high_ref[...] = vh
    low_ref[...] = vl
    for (some, part), (eh, el) in zip(halves(heads, width), parts):
        high = vh[:, part]
        wide = dg(jnp.concatenate([eh, el], axis=1), jnp.concatenate([high, high], axis=0), NN)
        wide = wide + dg(eh, vl[:, part], NN)
        wide = jnp.where(mask, wide.reshape(queries, half, width // 2), 0.0)
        acc_ref[:, part] = jnp.sum(wide, axis=1)


def delta_kernel(
    back, gate, high, low, expo, acc, stat, pay_ref, dprobs_ref, dctx
):
    back_ref, gate_ref, acc_ref, stat_ref = [v.ready() for v in (back, gate, acc, stat)]
    high_ref, low_ref, expo_ref = [v.ready() for v in (high, low, expo)]
    n_col, _, block = back_ref.shape
    queries, heads, keys = expo_ref.shape
    width = dctx.shape[1]
    for k in range(n_col):
        part = slice(k * block, (k + 1) * block)
        dctx[:, part] = back_ref[k] * gate_ref[:, part]
        pay_ref[k, :, :block] = acc_ref[:, part]
        pay_ref[k, :, block : block + heads] = stat_ref[:, :heads]
    half = heads // 2
    mask = head_mask(half, width // 2)[None]
    eye = eye_mask(half)[None]
    for some, part in halves(heads, width):
        dp = against(dctx[:, part], mask, high_ref[:, part], low_ref[:, part])
        dp = dp.reshape(queries, half, keys)
        dprobs_ref[:, some] = dp
        delta = jnp.sum(expo_ref[:, some] * dp, axis=-1, keepdims=True)
        first = 2 * heads + some.start
        delta = jnp.sum(jnp.where(eye, delta, 0.0), axis=1) * stat_ref[:, first : first + half]
        first = block + heads + some.start
        for k in range(n_col):
            pay_ref[k, :, first : first + half] = delta


def moment_kernel(
    x_far, expo_far, dprobs_far, rs_a, rs_b, out_far, x_ref, expo_ref, dprobs_ref, out_ref, sems
):
    heads = expo_ref.shape[1]
    chans = out_ref.shape[2]
    take = [
        Stream(x_far, x_ref, sems.at[0]),
        Stream(expo_far, expo_ref, sems.at[1], 1),
        Stream(dprobs_far, dprobs_ref, sems.at[2], 1),
    ]
    give = Stream(out_ref, out_far, sems.at[3], 2)
    for t in reversed(take):
        t.start()
    for t in take[1:]:
        t.wait()
    half = expo_ref.shape[0] // 2

    def step(rs_ref, shift, k, carry):
        take[0].copy(k).wait()
        for j in range(take[0].rows):
            i = k * take[0].rows + j
            e = expo_ref[i] * rs_ref[pl.ds(i - shift, 1), :]
            bh, bl = split(jnp.concatenate([e * dprobs_ref[i], e], axis=0))
            d2 = jnp.concatenate(split(centred(x_ref[i])), axis=1)
            wide = dg(jnp.concatenate([bh, bl], axis=0), d2, NN)
            high = wide[: 2 * heads]
            out_ref[i] = high[:, :chans] + high[:, chans:] + wide[2 * heads :, :chans]
        return carry

    lax.fori_loop(0, PARTS // 2, functools.partial(step, rs_a.ready(), 0), 0)
    give.copy(0).start()
    lax.fori_loop(PARTS // 2, PARTS, functools.partial(step, rs_b.ready(), half), 0)
    give.copy(1).start()
    give.wait()


def join_kernel(recv_ref, stat_ref, moment_ref, pgain_ref, pay_ref, join_ref):
    n, rows, lanes = recv_ref.shape
    heads = moment_ref.shape[1] // 2
    block = lanes - 2 * heads
    size = n * block // heads
    lane = lax.broadcasted_iota(jnp.int32, (heads, block), 1) + lax.axis_index("col") * block
    row = lax.broadcasted_iota(jnp.int32, (heads, block), 0) * size
    sel = jnp.where((lane >= row) & (lane < row + size), 1.0, 0.0)
    lse = [recv_ref[k, :, block : block + heads] for k in range(n)]
    top = functools.reduce(jnp.maximum, lse)
    weight = [jnp.exp(v - top) for v in lse]
    total = sum(weight)
    inv = 1.0 / total
    weight = [w * inv for w in weight]
    delta = sum(w * recv_ref[k, :, block + heads :] for k, w in enumerate(weight))
    fac = jnp.exp(stat_ref[:, heads : 2 * heads] - (top + jnp.log(total)))
    join_ref[:, :heads] = fac
    join_ref[:, heads : 2 * heads] = delta
    context = sum(
        lax.dot_general(w, sel, NN, precision=lax.Precision.HIGHEST, preferred_element_type=F32)
        * recv_ref[k, :, :block]
        for k, w in enumerate(weight)
    )
    eye = eye_mask(heads)[None]

    def column(v):
        return jnp.sum(jnp.where(eye, v[:, None, :], 0.0), axis=-1, keepdims=True)

    part = jnp.sum(
        column(fac) * moment_ref[:, :heads] - column(fac * delta) * moment_ref[:, heads:], axis=0
    ) * pgain_ref[...]
    for k in range(n):
        pay_ref[k, :rows, :block] = context
        pay_ref[k, rows:, :] = part


def grad_kernel(
    part, x_far, expo_far, dprobs_far, bias_far, rs, joined, wb, pgain, *refs
):
    out_far, x_ref, expo_ref, dprobs_ref, bias_ref, fac_ref, dlt_ref, out_ref, sems = refs[-9:]
    count, keys = out_ref.shape[:2]
    shift = part * count
    parts = PARTS // 2
    take = [
        Stream(x_far, x_ref, sems.at[0], parts, shift),
        Stream(expo_far, expo_ref, sems.at[1], 1, shift),
        Stream(dprobs_far, dprobs_ref, sems.at[2], 1, shift),
        Stream(bias_far, bias_ref, sems.at[3], 1),
    ]
    give = Stream(out_ref, out_far, sems.at[4], parts, shift)
    for t in reversed(take):
        t.start()
    heads = expo_ref.shape[1]
    chans = out_ref.shape[2]
    eye = eye_mask(heads)
    wt = centred(wb.ready()[...] * pgain.ready()[...])
    join_ref = joined.ready()
    rs_ref = rs.ready()
    zero = jnp.zeros_like(wt)
    mean = jnp.full_like(wt, 1.0 / chans)
    wh, wl = split(
        jnp.concatenate(
            [jnp.concatenate([wt, zero], axis=1), jnp.concatenate([zero, mean], axis=1)], axis=0
        )
    )

    def spread(w):
        nil = jnp.zeros_like(w)
        rows = [
            jnp.concatenate([w if m == n else nil for n in range(GROUP)], axis=1)
            for m in range(GROUP)
        ]
        return jnp.concatenate(rows, axis=0)

    weights = jnp.concatenate([spread(wh), spread(wh)], axis=0)
    rest = spread(wl)
    mask = eye[None]

    def columns(first):
        value = join_ref[pl.ds(shift, count), first : first + heads]
        value = jnp.where(mask, value[:, None, :], 0.0).reshape(count * heads, heads)
        high, rest = split(value)
        low, least = split(value - high.astype(F32))
        ones = jnp.ones((3 * heads, keys), BF16)
        return dg(jnp.concatenate([high, low, least], axis=1), ones, NN).reshape(count, heads, keys)

    fac_ref[...] = columns(0)
    dlt_ref[...] = columns(heads)
    for t in take[1:]:
        t.wait()

    def cells(i):
        rs = rs_ref[pl.ds(i, 1), :]
        u = expo_ref[i] * fac_ref[i] * (dprobs_ref[i] - dlt_ref[i]) * rs
        return [u, u * bias_ref[i] * rs]

    def step(k, carry):
        take[0].copy(k).wait()
        for j in range(0, give.rows, GROUP):
            first = k * give.rows + j
            rows = [part for m in range(GROUP) for part in cells(first + m)]
            high, low = split(jnp.concatenate(rows, axis=0).T)
            wide = dg(jnp.concatenate([high, low], axis=1), weights, NN) + dg(high, rest, NN)
            for m in range(GROUP):
                one = wide[:, 2 * chans * m : 2 * chans * (m + 1)]
                i = first + m
                out_ref[i] = one[:, :chans] - centred(x_ref[i]) * one[:, chans:]
        give.copy(k).start()
        return carry

    lax.fori_loop(0, parts, step, 0)
    give.wait()


def share_kernel(recv_ref, pay_ref):
    heads = pay_ref.shape[1]
    rows = recv_ref.shape[1] - heads
    total = recv_ref[0, rows:, :]
    for k in range(1, recv_ref.shape[0]):
        total = total + recv_ref[k, rows:, :]
    for k in range(pay_ref.shape[0]):
        pay_ref[k] = total


def out_kernel(recv_ref, gate_ref, wout_ref, att_ref, gated):
    rows, block = att_ref.shape
    for k in range(recv_ref.shape[0]):
        part = slice(k * block, (k + 1) * block)
        gated[:, part] = recv_ref[k, :rows, :block] * gate_ref[:, part]
    att_ref[...] = dot3(gated[...], wout_ref[...], NT)


def last_kernel(recv_ref, out_ref):
    total = recv_ref[0]
    for k in range(1, recv_ref.shape[0]):
        total = total + recv_ref[k]
    out_ref[...] = total


def place(col, owner, core):
    high, x = col // 4, col % 4
    y, low = owner // 2, owner % 2
    spot = (y + 6 - x + owner % 4) % 4
    near = lax.select(high == owner // 4, low, 1 - low) if not isinstance(owner, int) else (
        low if high == owner // 4 else 1 - low
    )
    return (spot * 2 + near) * 2 + core


def swap(x, axis):
    return lax.all_to_all(x, axis, 0, 0, tiled=True)


def local(
    single, pair, single_gain, pair_gain, w_query, w_key, w_value, w_gate, w_bias, w_out, cotangent
):
    n_row, n_col = lax.axis_size("row"), lax.axis_size("col")
    queries, keys, chans = pair.shape
    heads = w_bias.shape[1]
    width = single_gain.shape[0]
    block = single.shape[1]
    per = n_row // n_col
    gain = single_gain.reshape(-1, chans)
    pgain = pair_gain[None]
    wb = w_bias.T
    wout = w_out.T
    dma = pltpu.SemaphoreType.DMA
    shape_e = sds(queries, heads, keys)

    def mem(shape):
        return pltpu.VMEM(shape.shape, shape.dtype)

    perm = [
        (r * n_col + c, place(c, r // per, r % per) * n_col + r // per)
        for r in range(n_row)
        for c in range(n_col)
    ]
    moved = lax.ppermute(single, ("row", "col"), perm)
    pay1 = call(
        first_kernel,
        sds(n_col, queries + queries // 2, chans),
        2 * queries * width * block * 3,
        (single, cotangent, wout),
    )
    recv1 = swap(pay1, "col")
    shape_x = sds(queries, keys, chans)
    half_e = sds(queries // 2, heads, keys)
    half_rs = sds(queries // 2, keys)
    half_x = sds(queries // 2, keys, chans)
    held = [mem(half_x), mem(half_e), mem(half_rs), dma((3, PARTS // 2))]
    bias_a, rs_a = call(
        pair_kernel,
        (half_e, half_rs),
        queries * keys * chans * 200,
        (pair, wb, pgain),
        held,
        (0, 1, 1),
        (1, 1),
    )
    moved, rs_a = lax.optimization_barrier((moved, rs_a))
    recv2 = swap(jnp.broadcast_to(moved[None], (n_row,) + moved.shape), "row")
    square = pltpu.VMEM((width, width), F32)
    bias_b, rs_b, back_pay, query, gate = call(
        query_kernel,
        (
            half_e,
            half_rs,
            sds(n_col, queries, block),
            sds(queries, width),
            sds(queries, width),
        ),
        queries * keys * chans * 200 + queries * width * width * 12,
        (pair, wb, pgain, recv1, gain, w_query, w_gate),
        held + [pltpu.VMEM((queries, width), F32), square, square, dma((3,)), dma((3,))],
        (0, 1, 1, 1, 1, 0, 0),
        (1, 1, 0, 0, 0),
    )
    back = swap(back_pay, "col")
    vhigh, vlow, expo, acc, stat = call(
        score_kernel,
        (
            sds(keys, width, dtype=BF16),
            sds(keys, width, dtype=BF16),
            shape_e,
            sds(queries, width),
            sds(queries, chans),
        ),
        keys * width * width * 12,
        (recv2, gain, w_key, w_value, query, bias_a, bias_b),
        [pltpu.VMEM((keys, width), F32), square, square, dma((3,)), dma((3,))],
        (1, 1, 0, 0, 1, 1, 1),
    )
    pay4, dprobs = call(
        delta_kernel,
        (sds(n_col, queries, chans), shape_e),
        queries * keys * width * 12,
        (back, gate, vhigh, vlow, expo, acc, stat),
        [pltpu.VMEM((queries, width), F32)],
        (1,) * 7,
    )
    recv4 = swap(pay4, "col")
    shape_m = sds(queries, 2 * heads, chans)
    moment = call(
        moment_kernel,
        shape_m,
        queries * keys * chans * heads * 12,
        (pair, expo, dprobs, rs_a, rs_b),
        [mem(shape_x), mem(shape_e), mem(shape_e), mem(shape_m), dma((4, PARTS))],
        (0, 0, 0, 1, 1),
        (1,),
    )
    pay5, joined = call(
        join_kernel,
        (sds(n_col, queries + heads, chans), sds(queries, chans)),
        queries * heads * chans * 8,
        (recv4, stat, moment, pgain),
    )
    recv5 = swap(pay5, "col")
    cost = queries * keys * chans * 200
    held = [mem(half_x)] + 5 * [mem(half_e)] + [mem(half_x), dma((5, PARTS // 2))]
    place_of = (0, 0, 0, 0, 1, 1, 1, 1)
    first = call(
        functools.partial(grad_kernel, 0),
        shape_x,
        cost,
        (pair, expo, dprobs, bias_a, rs_a, joined, wb, pgain),
        held,
        place_of,
        (1,),
    )
    recv5, first = lax.optimization_barrier((recv5, first))
    pay6 = call(
        share_kernel, sds(n_row, heads, chans), queries * width, (recv5,), vmem=4 * MIB
    )
    recv6 = swap(pay6, "row")
    pair_grad = call(
        functools.partial(grad_kernel, 1),
        shape_x,
        cost,
        (pair, expo, dprobs, bias_b, rs_b, joined, wb, pgain, first),
        held,
        place_of + (0,),
        (1,),
        {8: 0},
    )
    attended = call(
        out_kernel,
        sds(queries, block),
        queries * width * block * 6,
        (recv5, gate, wout),
        [pltpu.VMEM((queries, width), F32)],
    )
    recv6, pair_grad, attended = lax.optimization_barrier((recv6, pair_grad, attended))
    bias_grad = call(last_kernel, sds(heads, chans), chans * heads, (recv6,), vmem=4 * MIB)
    return attended, pair_grad, bias_grad.T


def solution(mesh):
    placed = (
        P("row", "col"),
        P("row", "col", None),
        P(),
        P(),
        P(),
        P(),
        P(),
        P(),
        P(),
        P(None, "col"),
        P("row", "col"),
    )
    return jax.shard_map(
        local,
        mesh=mesh,
        in_specs=placed,
        out_specs=(P("row", "col"), P("row", "col", None), P()),
        check_vma=False,
    )
```

```python
import functools

import jax
import jax.numpy as jnp
from jax import lax
from jax.experimental import pallas as pl
from jax.experimental.pallas import tpu as pltpu
from jax.sharding import PartitionSpec as P

F32 = jnp.float32
BF16 = jnp.bfloat16
EPS = 1e-05
NN = (((1,), (0,)), ((), ()))
NT = (((1,), (1,)), ((), ()))
TN = (((0,), (0,)), ((), ()))
MIB = 1024 * 1024
VMEM_BYTES = 60 * MIB
PARTS = 4
GROUP = 4
LARGE = 48
FAR = pl.BlockSpec(memory_space=pl.ANY)
NEAR = pl.BlockSpec(memory_space=pltpu.VMEM)


def split(x):
    high = x.astype(BF16)
    return high, (x - high.astype(F32)).astype(BF16)


def dg(a, b, dims):
    return lax.dot_general(a, b, dims, preferred_element_type=F32)


def dot3(a, b, dims):
    ah, al = split(a)
    bh, bl = split(b)
    return dg(ah, bh, dims) + dg(al, bh, dims) + dg(ah, bl, dims)


class Near:
    def __init__(self, src, dst, sem):
        self.copy = pltpu.make_async_copy(src, dst, sem)
        self.copy.start()
        self.dst = dst
        self.waiting = True

    def ready(self):
        if self.waiting:
            self.copy.wait()
            self.waiting = False
        return self.dst


def call(kernel, out_shape, flops, args, scratch=(), near=None, far_out=None, alias=None, vmem=VMEM_BYTES):
    nbytes = sum(a.size * a.dtype.itemsize for a in args)
    for o in jax.tree.leaves(out_shape):
        nbytes += o.size * jnp.dtype(o.dtype).itemsize
    kw = {} if alias is None else {"input_output_aliases": alias}
    scratch = list(scratch)
    body = kernel
    if near is not None:
        kw["in_specs"] = [FAR] * len(args)
        small = [k for k, yes in enumerate(near) if yes]
        scratch += [pltpu.VMEM(args[k].shape, args[k].dtype) for k in small]
        scratch.append(pltpu.SemaphoreType.DMA((len(small),)))

        def body(*refs):
            refs = list(refs)
            places = refs[-len(small) - 1 : -1]
            for n, (k, place_) in enumerate(zip(small, places)):
                refs[k] = Near(refs[k], place_, refs[-1].at[n])
            kernel(*refs[: -len(small) - 1])

    if far_out is not None:
        specs = tuple(FAR if far else NEAR for far in far_out)
        kw["out_specs"] = specs if isinstance(out_shape, tuple) else specs[0]
    return pl.pallas_call(
        body,
        out_shape=out_shape,
        scratch_shapes=scratch,
        compiler_params=pltpu.CompilerParams(vmem_limit_bytes=vmem),
        cost_estimate=pl.CostEstimate(flops=flops, bytes_accessed=nbytes, transcendentals=0),
        **kw,
    )(*args)


class Stream:
    def __init__(self, src, dst, sems, parts=PARTS, shift=0):
        self.src, self.dst, self.sems, self.parts = src, dst, sems, parts
        self.rows = min(src.shape[0], dst.shape[0]) // parts
        self.src_shift = shift if src.shape[0] > dst.shape[0] else 0
        self.dst_shift = shift if src.shape[0] < dst.shape[0] else 0

    def copy(self, k):
        first = pl.multiple_of(k * self.rows, self.rows)
        there = pl.ds(first + self.src_shift, self.rows)
        here = pl.ds(first + self.dst_shift, self.rows)
        return pltpu.make_async_copy(self.src.at[there], self.dst.at[here], self.sems.at[k])

    def start(self):
        for k in range(self.parts):
            self.copy(k).start()

    def wait(self):
        for k in range(self.parts):
            self.copy(k).wait()


def sds(*shape, dtype=F32):
    return jax.ShapeDtypeStruct(shape, dtype)


def head_mask(heads, width):
    lane = lax.broadcasted_iota(jnp.int32, (heads, width), 1)
    row = lax.broadcasted_iota(jnp.int32, (heads, width), 0)
    size = width // heads
    return (lane >= row * size) & (lane < (row + 1) * size)


def eye_mask(n):
    return lax.broadcasted_iota(jnp.int32, (n, n), 0) == lax.broadcasted_iota(jnp.int32, (n, n), 1)


def first_kernel(single_ref, cot_ref, wout_ref, out_ref):
    n, _, lanes = out_ref.shape
    rows, block = single_ref.shape
    rest = lanes - block
    half = rows // 2
    single = single_ref[...]
    ch, cl = split(cot_ref[...])
    wh, wl = split(wout_ref[...])
    two = dg(jnp.concatenate([ch, cl], axis=0), wh, NN)
    full = two[:rows] + two[rows:] + dg(ch, wl, NN)
    for k in range(n):
        part = full[:, k * block : (k + 1) * block]
        out_ref[k, :rows, :block] = single
        out_ref[k, :rows, block:] = part[:, :rest]
        out_ref[k, rows:, : block - rest] = part[:half, rest:]
        out_ref[k, rows:, block - rest :] = part[half:, rest:]


def joined_norm(blocks, out_ref, row):
    rows, block = blocks[0].shape
    width = block * len(blocks)
    centre = sum(jnp.sum(b, axis=-1, keepdims=True) for b in blocks) / width
    blocks = [b - centre for b in blocks]
    spread = sum(jnp.sum(b * b, axis=-1, keepdims=True) for b in blocks) / width
    scale = lax.rsqrt(spread + EPS)
    for k, b in enumerate(blocks):
        part = slice(k * block, (k + 1) * block)
        out_ref[row : row + rows, part] = b * scale


def gained(normed, gain_ref):
    tiles, lanes = gain_ref.shape
    parts = [
        split(normed[:, t * lanes : (t + 1) * lanes] * gain_ref[t : t + 1, :]) for t in range(tiles)
    ]
    return jnp.concatenate(
        [jnp.concatenate([p[k] for p in parts], axis=1) for k in range(2)], axis=0
    )


def project(both, weight, copies):
    rows = both.shape[0] // 2
    third = weight.shape[0] // 3
    out = None
    for k, one in enumerate(copies):
        one.wait()
        here = slice(k * third, (k + 1) * third)
        wh, wl = split(weight[here, :])
        two = dg(both[:, here], wh, NN)
        part = two[:rows] + two[rows:] + dg(both[:rows, here], wl, NN)
        out = part if out is None else out + part
    return out


def fetch(src, dst, sems):
    rows = src.shape[0] // 3
    out = []
    for k in range(3):
        here = pl.ds(k * rows, rows)
        one = pltpu.make_async_copy(src.at[here], dst.at[here], sems.at[k])
        one.start()
        out.append(one)
    return out


def back_kernel(recv_ref, back_ref):
    rows, block = back_ref.shape
    total = recv_ref[0]
    for k in range(1, recv_ref.shape[0]):
        total = total + recv_ref[k]
    rest = total.shape[1] - block
    right = jnp.concatenate([total[rows:, : block - rest], total[rows:, block - rest :]], axis=0)
    total = jnp.concatenate([total[:rows, block:], right], axis=1)
    back_ref[...] = total


def query_kernel(
    pair_far, wb, pgain, recv, gain, wq_far, wg_far,
    bias_far, rs_far, query_ref, gate_ref,
    x_ref, bias_ref, rs_ref, sems, normed, wq, wg, qsem, gsem,
):
    take, give = bias_streams(pair_far, bias_far, rs_far, x_ref, bias_ref, rs_ref, sems, 1)
    query_copies = fetch(wq_far, wq, qsem)
    gate_copies = fetch(wg_far, wg, gsem)
    bias_rows(take, give, wb.ready(), pgain.ready(), x_ref, bias_ref, rs_ref)
    recv_ref = recv.ready()
    n = recv_ref.shape[0]
    rows, width = query_ref.shape
    joined_norm([recv_ref[k, :rows, : width // n] for k in range(n)], normed, 0)
    both = gained(normed, gain.ready())
    query_ref[...] = project(both, wq, query_copies) * (48 ** -0.5)
    gate_ref[...] = 1.0 / (1.0 + jnp.exp(-project(both, wg, gate_copies)))
    for g in give:
        g.wait()


def centred(x):
    return x - jnp.sum(x, axis=-1, keepdims=True) * (1.0 / x.shape[-1])


def bias_streams(pair_far, bias_far, rs_far, x_ref, bias_ref, rs_ref, sems, part):
    parts = PARTS // 2
    take = Stream(pair_far, x_ref, sems.at[0], parts, part * LARGE)
    take.start()
    return take, [Stream(bias_ref, bias_far, sems.at[1], 1), Stream(rs_ref, rs_far, sems.at[2], 1)]


def bias_rows(take, give, wb_ref, pgain_ref, x_ref, bias_ref, rs_ref):
    chans = x_ref.shape[2]
    heads = bias_ref.shape[1]
    wh, wl = split(wb_ref[...] * pgain_ref[...])
    top = jnp.concatenate([wh, wh], axis=1)
    left = jnp.concatenate([top, jnp.concatenate([wl, jnp.zeros_like(wl)], axis=1)], axis=0)
    ones = jnp.ones((8, 2 * chans), BF16)

    def step(k, carry):
        take.copy(k).wait()
        for j in range(take.rows):
            i = k * take.rows + j
            d = centred(x_ref[i])
            spread = dg(ones, jnp.concatenate(split(d * d), axis=1), NT) * (1.0 / chans)
            rs = lax.rsqrt(spread[0:1] + EPS)
            two = dg(left, jnp.concatenate(split(d), axis=1), NT)
            bias_ref[i] = (two[:heads] + two[heads:]) * rs
            rs_ref[pl.ds(i, 1), :] = rs
        return carry

    lax.fori_loop(0, take.parts, step, 0)
    for g in give:
        g.start()


def pair_kernel(pair_far, wb, pgain, bias_far, rs_far, x_ref, bias_ref, rs_ref, sems):
    take, give = bias_streams(pair_far, bias_far, rs_far, x_ref, bias_ref, rs_ref, sems, 0)
    bias_rows(take, give, wb.ready(), pgain.ready(), x_ref, bias_ref, rs_ref)
    for g in give:
        g.wait()


def halves(heads, width):
    return [
        (slice(g * heads // 2, (g + 1) * heads // 2), slice(g * width // 2, (g + 1) * width // 2))
        for g in range(2)
    ]


def by_head(rows, mask):
    wide = jnp.where(mask, rows[:, None, :], 0.0)
    return split(wide.reshape(-1, rows.shape[1]))


def against(rows, mask, high, low):
    keys = high.shape[0]
    rh, rl = by_head(rows, mask)
    two = dg(rh, jnp.concatenate([high, low], axis=0), NT)
    return two[:, :keys] + two[:, keys:] + dg(rl, high, NT)


def attend_kernel(
    own, far_a, far_b, far_c, gain, wk_far, wv_far, query, bias_a, bias_b, back_four, back_far, gate,
    pay_ref, expo_ref, dprobs_ref, stat_ref,
    normed, wk, wv, dctx, acc, ksem, vsem,
):
    key_copies = fetch(wk_far, wk, ksem)
    value_copies = fetch(wv_far, wv, vsem)
    blocks = [piece.ready() for piece in (own, far_a, far_b, far_c)]
    n_sub, rows, block = blocks[0].shape
    queries, heads, keys = expo_ref.shape
    width = normed.shape[1]
    n_col = width // block
    me = lax.axis_index("row")
    col = lax.axis_index("col")

    def token_block(k, core):
        there = place(k, col, core)
        hop = (me // n_sub + 4 - there // n_sub) % 4
        spot = (me % n_sub) ^ (there % n_sub)
        some = [piece[spot] for piece in blocks]
        return jnp.where(
            hop < 2, jnp.where(hop == 0, some[0], some[1]), jnp.where(hop == 2, some[2], some[3])
        )

    for t in range(keys // rows):
        joined_norm([token_block(k, t) for k in range(n_col)], normed, t * rows)
    both = gained(normed, gain.ready())
    kh, kl = split(project(both, wk, key_copies))
    half = heads // 2
    mask = head_mask(half, width // 2)[None]
    eye = eye_mask(half)[None]

    def lanes(column):
        return jnp.sum(jnp.where(eye, column.reshape(queries, half, 1), 0.0), axis=1)

    parts = []
    query_ref = query.ready()
    bias_refs = [bias_a.ready(), bias_b.ready()]
    for some, part in halves(heads, width):
        bias = jnp.concatenate([b[:, some] for b in bias_refs], axis=0)
        scores = against(query_ref[:, part], mask, kh[:, part], kl[:, part])
        scores = scores + bias.reshape(queries * half, keys)
        top = jnp.max(scores, axis=-1, keepdims=True)
        expo = jnp.exp(scores - top)
        total = jnp.sum(expo, axis=-1, keepdims=True)
        expo_ref[:, some] = expo.reshape(queries, half, keys)
        stat_ref[:, some] = lanes(top)
        lse = lanes(top + jnp.log(total))
        for k in range(n_col):
            pay_ref[k, :, block + some.start : block + some.stop] = lse
        parts.append(expo * (1.0 / total))
    vh, vl = split(project(both, wv, value_copies))
    backs, gate_ref = [back_four.ready(), back_far.ready()], gate.ready()
    n_x = backs[0].shape[0]
    for k in range(n_col):
        part = slice(k * block, (k + 1) * block)
        spot = (col + n_x - k) % n_x
        near = col // n_x == k // n_x
        dctx[:, part] = jnp.where(near, backs[0][spot], backs[1][spot]) * gate_ref[:, part]
    for (some, part), probs in zip(halves(heads, width), parts):
        high, low = vh[:, part], vl[:, part]
        eh, el = split(probs)
        wide = dg(jnp.concatenate([eh, el], axis=1), jnp.concatenate([high, high], axis=0), NN)
        wide = wide + dg(eh, low, NN)
        wide = jnp.where(mask, wide.reshape(queries, half, width // 2), 0.0)
        acc[:, part] = jnp.sum(wide, axis=1)
        dp = against(dctx[:, part], mask, high, low)
        dprobs_ref[:, some] = dp.reshape(queries, half, keys)
        delta = lanes(jnp.sum(probs * dp, axis=-1, keepdims=True))
        for k in range(n_col):
            pay_ref[k, :, block + heads + some.start : block + heads + some.stop] = delta
    for k in range(n_col):
        pay_ref[k, :, :block] = acc[:, k * block : (k + 1) * block]


def moment_kernel(
    x_far, expo_far, dprobs_far, rs_a, rs_b, out_far, x_ref, expo_ref, dprobs_ref, out_ref, sems
):
    heads = expo_ref.shape[1]
    chans = out_ref.shape[2]
    take = [
        Stream(x_far, x_ref, sems.at[0]),
        Stream(expo_far, expo_ref, sems.at[1], 1),
        Stream(dprobs_far, dprobs_ref, sems.at[2], 1),
    ]
    give = Stream(out_ref, out_far, sems.at[3])
    for t in reversed(take):
        t.start()
    for t in take[1:]:
        t.wait()
    cut = PARTS * LARGE // expo_ref.shape[0]

    def step(rs_ref, shift, k, carry):
        take[0].copy(k).wait()
        for j in range(take[0].rows):
            i = k * take[0].rows + j
            e = expo_ref[i] * rs_ref[pl.ds(i - shift, 1), :]
            bh, bl = split(jnp.concatenate([e * dprobs_ref[i], e], axis=0))
            d2 = jnp.concatenate(split(centred(x_ref[i])), axis=1)
            wide = dg(jnp.concatenate([bh, bl], axis=0), d2, NN)
            high = wide[: 2 * heads]
            out_ref[i] = high[:, :chans] + high[:, chans:] + wide[2 * heads :, :chans]
        return carry

    lax.fori_loop(0, cut, functools.partial(step, rs_a.ready(), 0), 0)
    for k in range(cut):
        give.copy(k).start()
    lax.fori_loop(cut, PARTS, functools.partial(step, rs_b.ready(), LARGE), 0)
    for k in range(cut, PARTS):
        give.copy(k).start()
    give.wait()


def join_kernel(recv_ref, stat_ref, moment_ref, pgain_ref, pay_ref, join_ref):
    n, rows, lanes = recv_ref.shape
    heads = moment_ref.shape[1] // 2
    block = lanes - 2 * heads
    size = n * block // heads
    lane = lax.broadcasted_iota(jnp.int32, (heads, block), 1) + lax.axis_index("col") * block
    row = lax.broadcasted_iota(jnp.int32, (heads, block), 0) * size
    sel = jnp.where((lane >= row) & (lane < row + size), 1.0, 0.0)
    lse = [recv_ref[k, :, block : block + heads] for k in range(n)]
    top = functools.reduce(jnp.maximum, lse)
    weight = [jnp.exp(v - top) for v in lse]
    total = sum(weight)
    inv = 1.0 / total
    weight = [w * inv for w in weight]
    delta = sum(w * recv_ref[k, :, block + heads :] for k, w in enumerate(weight))
    fac = jnp.exp(stat_ref[:, :heads] - (top + jnp.log(total)))
    join_ref[:, :heads] = fac
    join_ref[:, heads : 2 * heads] = delta
    context = sum(
        lax.dot_general(w, sel, NN, precision=lax.Precision.HIGHEST, preferred_element_type=F32)
        * recv_ref[k, :, :block]
        for k, w in enumerate(weight)
    )
    eye = eye_mask(heads)[None]

    def column(v):
        return jnp.sum(jnp.where(eye, v[:, None, :], 0.0), axis=-1, keepdims=True)

    part = jnp.sum(
        column(fac) * moment_ref[:, :heads] - column(fac * delta) * moment_ref[:, heads:], axis=0
    ) * pgain_ref[...]
    for k in range(n):
        pay_ref[k, :rows, :block] = context
        pay_ref[k, rows:, :] = part


def grad_kernel(
    part, x_far, expo_far, dprobs_far, bias_far, rs, joined, wb, pgain, *refs
):
    out_far, x_ref, expo_ref, dprobs_ref, bias_ref, fac_ref, dlt_ref, out_ref, sems = refs[-9:]
    count, keys = out_ref.shape[:2]
    shift = part * LARGE
    parts = PARTS // 2
    take = [
        Stream(x_far, x_ref, sems.at[0], parts, shift),
        Stream(expo_far, expo_ref, sems.at[1], 1, shift),
        Stream(dprobs_far, dprobs_ref, sems.at[2], 1, shift),
        Stream(bias_far, bias_ref, sems.at[3], 1),
    ]
    give = Stream(out_ref, out_far, sems.at[4], parts, shift)
    for t in reversed(take):
        t.start()
    heads = expo_ref.shape[1]
    chans = out_ref.shape[2]
    eye = eye_mask(heads)
    wt = centred(wb.ready()[...] * pgain.ready()[...])
    join_ref = joined.ready()
    rs_ref = rs.ready()
    zero = jnp.zeros_like(wt)
    mean = jnp.full_like(wt, 1.0 / chans)
    wh, wl = split(
        jnp.concatenate(
            [jnp.concatenate([wt, zero], axis=1), jnp.concatenate([zero, mean], axis=1)], axis=0
        )
    )

    def spread(w):
        nil = jnp.zeros_like(w)
        rows = [
            jnp.concatenate([w if m == n else nil for n in range(GROUP)], axis=1)
            for m in range(GROUP)
        ]
        return jnp.concatenate(rows, axis=0)

    weights = jnp.concatenate([spread(wh), spread(wh)], axis=0)
    rest = spread(wl)
    mask = eye[None]

    def columns(first):
        value = join_ref[pl.ds(shift, count), first : first + heads]
        value = jnp.where(mask, value[:, None, :], 0.0).reshape(count * heads, heads)
        high, rest = split(value)
        low, least = split(value - high.astype(F32))
        ones = jnp.ones((3 * heads, keys), BF16)
        return dg(jnp.concatenate([high, low, least], axis=1), ones, NN).reshape(count, heads, keys)

    fac_ref[...] = columns(0)
    dlt_ref[...] = columns(heads)
    for t in take[1:]:
        t.wait()

    def cells(i):
        rs = rs_ref[pl.ds(i, 1), :]
        u = expo_ref[i] * fac_ref[i] * (dprobs_ref[i] - dlt_ref[i]) * rs
        return [u, u * bias_ref[i] * rs]

    def step(k, carry):
        take[0].copy(k).wait()
        for j in range(0, give.rows, GROUP):
            first = k * give.rows + j
            rows = [part for m in range(GROUP) for part in cells(first + m)]
            high, low = split(jnp.concatenate(rows, axis=0).T)
            wide = dg(jnp.concatenate([high, low], axis=1), weights, NN) + dg(high, rest, NN)
            for m in range(GROUP):
                one = wide[:, 2 * chans * m : 2 * chans * (m + 1)]
                i = first + m
                out_ref[i] = one[:, :chans] - centred(x_ref[i]) * one[:, chans:]
        give.copy(k).start()
        return carry

    lax.fori_loop(0, parts, step, 0)
    give.wait()


def share_kernel(recv_ref, pay_ref):
    heads = pay_ref.shape[1]
    rows = recv_ref.shape[1] - heads
    total = recv_ref[0, rows:, :]
    for k in range(1, recv_ref.shape[0]):
        total = total + recv_ref[k, rows:, :]
    for k in range(pay_ref.shape[0]):
        pay_ref[k] = total


def out_kernel(recv_ref, gate_ref, wout_ref, att_ref, gated):
    rows, block = att_ref.shape
    for k in range(recv_ref.shape[0]):
        part = slice(k * block, (k + 1) * block)
        gated[:, part] = recv_ref[k, :rows, :block] * gate_ref[:, part]
    att_ref[...] = dot3(gated[...], wout_ref[...], NT)


def last_kernel(recv_ref, out_ref):
    total = recv_ref[0]
    for k in range(1, recv_ref.shape[0]):
        total = total + recv_ref[k]
    out_ref[...] = total


def place(col, owner, core):
    high, x = col // 4, col % 4
    y, low = owner // 2, owner % 2
    spot = (y + 6 - x + owner % 4) % 4
    near = lax.select(high == owner // 4, low, 1 - low) if not isinstance(owner, int) else (
        low if high == owner // 4 else 1 - low
    )
    return (spot * 2 + near) * 2 + core


def swap(x, axis):
    return lax.all_to_all(x, axis, 0, 0, tiled=True)


def local(
    single, pair, single_gain, pair_gain, w_query, w_key, w_value, w_gate, w_bias, w_out, cotangent
):
    n_row, n_col = lax.axis_size("row"), lax.axis_size("col")
    queries, keys, chans = pair.shape
    heads = w_bias.shape[1]
    width = single_gain.shape[0]
    block = single.shape[1]
    per = n_row // n_col
    gain = single_gain.reshape(-1, chans)
    pgain = pair_gain[None]
    wb = w_bias.T
    wout = w_out.T
    dma = pltpu.SemaphoreType.DMA
    shape_e = sds(queries, heads, keys)

    def mem(shape):
        return pltpu.VMEM(shape.shape, shape.dtype)

    perm = [
        (r * n_col + c, place(c, r // per, r % per) * n_col + r // per)
        for r in range(n_row)
        for c in range(n_col)
    ]
    moved = lax.ppermute(single, ("row", "col"), perm)
    pay1 = call(
        first_kernel,
        sds(n_col, queries + queries // 2, chans),
        2 * queries * width * block * 3,
        (single, cotangent, wout),
    )
    recv1 = swap(pay1, "col")
    shape_x = sds(queries, keys, chans)
    counts = (LARGE, queries - LARGE)
    parts_e = [sds(n, heads, keys) for n in counts]
    parts_rs = [sds(n, keys) for n in counts]
    parts_x = [sds(n, keys, chans) for n in counts]
    held = [
        [mem(x), mem(e), mem(rs), dma((3, PARTS // 2))]
        for x, e, rs in zip(parts_x, parts_e, parts_rs)
    ]
    bias_a, rs_a = call(
        pair_kernel,
        (parts_e[0], parts_rs[0]),
        queries * keys * chans * 200,
        (pair, wb, pgain),
        held[0],
        (0, 1, 1),
        (1, 1),
    )
    moved, rs_a = lax.optimization_barrier((moved, rs_a))

    def along(x, target):
        return lax.ppermute(x, "row", [(r, target(r)) for r in range(n_row)])

    pair_of = jnp.stack([moved, along(moved, lambda r: r ^ 1)])
    back_pay = call(back_kernel, sds(queries, block), queries * width, (recv1,), vmem=4 * MIB)
    four = jnp.concatenate([pair_of, along(pair_of, lambda r: r ^ 2)])
    n_x = 4

    def around(x, k):
        return lax.ppermute(x, "col", [(c, c - c % n_x + (c + k) % n_x) for c in range(n_col)])

    back_four = jnp.stack([back_pay] + [around(back_pay, k) for k in range(1, n_x)])
    back_far = lax.ppermute(back_four, "col", [(c, (c + n_x) % n_col) for c in range(n_col)])
    ring = [along(four, lambda r: (r + 4 * k) % n_row) for k in range(1, 4)]
    recv1, four = lax.optimization_barrier((recv1, four))
    square = pltpu.VMEM((width, width), F32)
    bias_b, rs_b, query, gate = call(
        query_kernel,
        (
            parts_e[1],
            parts_rs[1],
            sds(queries, width),
            sds(queries, width),
        ),
        queries * keys * chans * 200 + queries * width * width * 12,
        (pair, wb, pgain, recv1, gain, w_query, w_gate),
        held[1] + [pltpu.VMEM((queries, width), F32), square, square, dma((3,)), dma((3,))],
        (0, 1, 1, 1, 1, 0, 0),
        (1, 1, 0, 0),
    )
    pay4, expo, dprobs, stat = call(
        attend_kernel,
        (sds(n_col, queries, chans), shape_e, shape_e, sds(queries, chans)),
        keys * width * width * 12,
        (four, *ring, gain, w_key, w_value, query, bias_a, bias_b, back_four, back_far, gate),
        [
            pltpu.VMEM((keys, width), F32),
            square,
            square,
            pltpu.VMEM((queries, width), F32),
            pltpu.VMEM((queries, width), F32),
            dma((3,)),
            dma((3,)),
        ],
        (1, 1, 1, 1, 1, 0, 0, 1, 1, 1, 1, 1, 1),
    )
    recv4 = swap(pay4, "col")
    shape_m = sds(queries, 2 * heads, chans)
    moment = call(
        moment_kernel,
        shape_m,
        queries * keys * chans * heads * 12,
        (pair, expo, dprobs, rs_a, rs_b),
        [mem(shape_x), mem(shape_e), mem(shape_e), mem(shape_m), dma((4, PARTS))],
        (0, 0, 0, 1, 1),
        (1,),
    )
    pay5, joined = call(
        join_kernel,
        (sds(n_col, queries + heads, chans), sds(queries, chans)),
        queries * heads * chans * 8,
        (recv4, stat, moment, pgain),
    )
    recv5 = swap(pay5, "col")
    cost = queries * keys * chans * 200
    held = [
        [mem(x)] + 5 * [mem(e)] + [mem(x), dma((5, PARTS // 2))] for x, e in zip(parts_x, parts_e)
    ]
    place_of = (0, 0, 0, 0, 1, 1, 1, 1)
    first = call(
        functools.partial(grad_kernel, 0),
        shape_x,
        cost,
        (pair, expo, dprobs, bias_a, rs_a, joined, wb, pgain),
        held[0],
        place_of,
        (1,),
    )
    recv5, first = lax.optimization_barrier((recv5, first))
    pay6 = call(
        share_kernel, sds(n_row, heads, chans), queries * width, (recv5,), vmem=4 * MIB
    )
    recv6 = swap(pay6, "row")
    pair_grad = call(
        functools.partial(grad_kernel, 1),
        shape_x,
        cost,
        (pair, expo, dprobs, bias_b, rs_b, joined, wb, pgain, first),
        held[1],
        place_of + (0,),
        (1,),
        {8: 0},
    )
    attended = call(
        out_kernel,
        sds(queries, block),
        queries * width * block * 6,
        (recv5, gate, wout),
        [pltpu.VMEM((queries, width), F32)],
    )
    recv6, pair_grad, attended = lax.optimization_barrier((recv6, pair_grad, attended))
    bias_grad = call(last_kernel, sds(heads, chans), chans * heads, (recv6,), vmem=4 * MIB)
    return attended, pair_grad, bias_grad.T


def solution(mesh):
    placed = (
        P("row", "col"),
        P("row", "col", None),
        P(),
        P(),
        P(),
        P(),
        P(),
        P(),
        P(),
        P(None, "col"),
        P("row", "col"),
    )
    return jax.shard_map(
        local,
        mesh=mesh,
        in_specs=placed,
        out_specs=(P("row", "col"), P("row", "col", None), P()),
        check_vma=False,
    )
```

```python
import functools

import jax
import jax.numpy as jnp
from jax import lax
from jax.experimental import pallas as pl
from jax.experimental.pallas import tpu as pltpu
from jax.sharding import PartitionSpec as P

F32 = jnp.float32
BF16 = jnp.bfloat16
EPS = 1e-05
NN = (((1,), (0,)), ((), ()))
NT = (((1,), (1,)), ((), ()))
TN = (((0,), (0,)), ((), ()))
MIB = 1024 * 1024
VMEM_BYTES = 60 * MIB
PARTS = 4
GROUP = 4
LANES = 128
LARGE = 48
FAR = pl.BlockSpec(memory_space=pl.ANY)
NEAR = pl.BlockSpec(memory_space=pltpu.VMEM)


def split(x):
    high = x.astype(BF16)
    return high, (x - high.astype(F32)).astype(BF16)


def dg(a, b, dims):
    return lax.dot_general(a, b, dims, preferred_element_type=F32)


def dot3(a, b, dims):
    ah, al = split(a)
    bh, bl = split(b)
    return dg(ah, bh, dims) + dg(al, bh, dims) + dg(ah, bl, dims)


class Near:
    def __init__(self, src, dst, sem):
        self.copy = pltpu.make_async_copy(src, dst, sem)
        self.dst = dst
        self.waiting = True

    def start(self):
        self.copy.start()
        return self

    def ready(self):
        if self.waiting:
            self.copy.wait()
            self.waiting = False
        return self.dst


def call(kernel, out_shape, flops, args, scratch=(), near=None, far_out=None, alias=None, vmem=VMEM_BYTES):
    nbytes = sum(a.size * a.dtype.itemsize for a in args)
    for o in jax.tree.leaves(out_shape):
        nbytes += o.size * jnp.dtype(o.dtype).itemsize
    kw = {} if alias is None else {"input_output_aliases": alias}
    scratch = list(scratch)
    body = kernel
    if near is not None:
        kw["in_specs"] = [FAR] * len(args)
        small = [k for k, yes in enumerate(near) if yes]
        scratch += [pltpu.VMEM(args[k].shape, args[k].dtype) for k in small]
        scratch.append(pltpu.SemaphoreType.DMA((len(small),)))

        def body(*refs):
            refs = list(refs)
            places = refs[-len(small) - 1 : -1]
            for n, (k, place_) in enumerate(zip(small, places)):
                refs[k] = Near(refs[k], place_, refs[-1].at[n])
                if near[k] == 1:
                    refs[k].start()
            kernel(*refs[: -len(small) - 1])

    if far_out is not None:
        specs = tuple(FAR if far else NEAR for far in far_out)
        kw["out_specs"] = specs if isinstance(out_shape, tuple) else specs[0]
    return pl.pallas_call(
        body,
        out_shape=out_shape,
        scratch_shapes=scratch,
        compiler_params=pltpu.CompilerParams(vmem_limit_bytes=vmem),
        cost_estimate=pl.CostEstimate(flops=flops, bytes_accessed=nbytes, transcendentals=0),
        **kw,
    )(*args)


class Stream:
    def __init__(self, src, dst, sems, parts=PARTS, shift=0):
        self.src, self.dst, self.sems, self.parts = src, dst, sems, parts
        self.rows = min(src.shape[0], dst.shape[0]) // parts
        self.src_shift = shift if src.shape[0] > dst.shape[0] else 0
        self.dst_shift = shift if src.shape[0] < dst.shape[0] else 0

    def copy(self, k):
        first = pl.multiple_of(k * self.rows, self.rows)
        there = pl.ds(first + self.src_shift, self.rows)
        here = pl.ds(first + self.dst_shift, self.rows)
        return pltpu.make_async_copy(self.src.at[there], self.dst.at[here], self.sems.at[k])

    def start(self):
        for k in range(self.parts):
            self.copy(k).start()

    def wait(self):
        for k in range(self.parts):
            self.copy(k).wait()


def sds(*shape, dtype=F32):
    return jax.ShapeDtypeStruct(shape, dtype)


def head_mask(heads, width):
    lane = lax.broadcasted_iota(jnp.int32, (heads, width), 1)
    row = lax.broadcasted_iota(jnp.int32, (heads, width), 0)
    size = width // heads
    return (lane >= row * size) & (lane < (row + 1) * size)


def eye_mask(n):
    return lax.broadcasted_iota(jnp.int32, (n, n), 0) == lax.broadcasted_iota(jnp.int32, (n, n), 1)


def first_kernel(single_ref, cot_ref, wout_ref, out_ref):
    n, _, lanes = out_ref.shape
    rows, block = single_ref.shape
    rest = lanes - block
    half = rows // 2
    single = single_ref[...]
    ch, cl = split(cot_ref[...])
    wh, wl = split(wout_ref[...])
    two = dg(jnp.concatenate([ch, cl], axis=0), wh, NN)
    full = two[:rows] + two[rows:] + dg(ch, wl, NN)
    for k in range(n):
        part = full[:, k * block : (k + 1) * block]
        out_ref[k, :rows, :block] = single
        out_ref[k, :rows, block:] = part[:, :rest]
        out_ref[k, rows:, : block - rest] = part[:half, rest:]
        out_ref[k, rows:, block - rest :] = part[half:, rest:]


def joined_norm(blocks, out_ref, row):
    rows, block = blocks[0].shape
    width = block * len(blocks)
    centre = sum(jnp.sum(b, axis=-1, keepdims=True) for b in blocks) / width
    blocks = [b - centre for b in blocks]
    spread = sum(jnp.sum(b * b, axis=-1, keepdims=True) for b in blocks) / width
    scale = lax.rsqrt(spread + EPS)
    for k, b in enumerate(blocks):
        part = slice(k * block, (k + 1) * block)
        out_ref[row : row + rows, part] = b * scale


def gained(normed, gain_ref):
    tiles, lanes = gain_ref.shape
    parts = [
        split(normed[:, t * lanes : (t + 1) * lanes] * gain_ref[t : t + 1, :]) for t in range(tiles)
    ]
    return jnp.concatenate(
        [jnp.concatenate([p[k] for p in parts], axis=1) for k in range(2)], axis=0
    )


def project(both, weight, copies):
    rows = both.shape[0] // 2
    third = weight.shape[0] // 3
    out = None
    for k, one in enumerate(copies):
        one.wait()
        here = slice(k * third, (k + 1) * third)
        wh, wl = split(weight[here, :])
        two = dg(both[:, here], wh, NN)
        part = two[:rows] + two[rows:] + dg(both[:rows, here], wl, NN)
        out = part if out is None else out + part
    return out


def fetch(src, dst, sems):
    rows = src.shape[0] // 3
    out = []
    for k in range(3):
        here = pl.ds(k * rows, rows)
        one = pltpu.make_async_copy(src.at[here], dst.at[here], sems.at[k])
        one.start()
        out.append(one)
    return out


def back_kernel(recv_ref, back_ref):
    rows, block = back_ref.shape
    total = recv_ref[0]
    for k in range(1, recv_ref.shape[0]):
        total = total + recv_ref[k]
    rest = total.shape[1] - block
    right = jnp.concatenate([total[rows:, : block - rest], total[rows:, block - rest :]], axis=0)
    total = jnp.concatenate([total[:rows, block:], right], axis=1)
    back_ref[...] = total


def query_kernel(
    pair_far, wb, pgain, recv, gain, wq_far, wg_far,
    bias_far, rs_far, query_ref, gate_ref,
    x_ref, bias_ref, rs_ref, sems, normed, wq, wg, qsem, gsem,
):
    take, give = bias_streams(pair_far, bias_far, rs_far, x_ref, bias_ref, rs_ref, sems, 1)
    query_copies = fetch(wq_far, wq, qsem)
    gate_copies = fetch(wg_far, wg, gsem)
    bias_rows(take, give, wb.ready(), pgain.ready(), x_ref, bias_ref, rs_ref)
    recv_ref = recv.ready()
    n = recv_ref.shape[0]
    rows, width = query_ref.shape
    joined_norm([recv_ref[k, :rows, : width // n] for k in range(n)], normed, 0)
    both = gained(normed, gain.ready())
    query_ref[...] = project(both, wq, query_copies) * (48 ** -0.5)
    gate_ref[...] = 1.0 / (1.0 + jnp.exp(-project(both, wg, gate_copies)))
    for g in give:
        g.wait()


def centred(x):
    return x - jnp.sum(x, axis=-1, keepdims=True) * (1.0 / x.shape[-1])


def bias_streams(pair_far, bias_far, rs_far, x_ref, bias_ref, rs_ref, sems, part):
    parts = PARTS // 2
    take = Stream(pair_far, x_ref, sems.at[0], parts, part * LARGE)
    take.start()
    return take, [Stream(bias_ref, bias_far, sems.at[1], 1), Stream(rs_ref, rs_far, sems.at[2], 1)]


def bias_rows(take, give, wb_ref, pgain_ref, x_ref, bias_ref, rs_ref):
    chans = x_ref.shape[2]
    heads = bias_ref.shape[1]
    wh, wl = split(wb_ref[...] * pgain_ref[...])
    top = jnp.concatenate([wh, wh], axis=1)
    left = jnp.concatenate([top, jnp.concatenate([wl, jnp.zeros_like(wl)], axis=1)], axis=0)
    ones = jnp.ones((8, 2 * chans), BF16)

    def step(k, carry):
        take.copy(k).wait()
        for j in range(take.rows):
            i = k * take.rows + j
            d = centred(x_ref[i])
            spread = dg(ones, jnp.concatenate(split(d * d), axis=1), NT) * (1.0 / chans)
            rs = lax.rsqrt(spread[0:1] + EPS)
            two = dg(left, jnp.concatenate(split(d), axis=1), NT)
            bias_ref[i] = (two[:heads] + two[heads:]) * rs
            rs_ref[pl.ds(i, 1), :] = rs
        return carry

    lax.fori_loop(0, take.parts, step, 0)
    for g in give:
        g.start()


def pair_kernel(pair_far, wb, pgain, bias_far, rs_far, x_ref, bias_ref, rs_ref, sems):
    take, give = bias_streams(pair_far, bias_far, rs_far, x_ref, bias_ref, rs_ref, sems, 0)
    bias_rows(take, give, wb.ready(), pgain.ready(), x_ref, bias_ref, rs_ref)
    for g in give:
        g.wait()


def halves(heads, width):
    return [
        (slice(g * heads // 2, (g + 1) * heads // 2), slice(g * width // 2, (g + 1) * width // 2))
        for g in range(2)
    ]


def by_head(rows, mask):
    wide = jnp.where(mask, rows[:, None, :], 0.0)
    return split(wide.reshape(-1, rows.shape[1]))


def against(rows, mask, high, low):
    keys = high.shape[0]
    rh, rl = by_head(rows, mask)
    two = dg(rh, jnp.concatenate([high, low], axis=0), NT)
    return two[:, :keys] + two[:, keys:] + dg(rl, high, NT)


def attend_kernel(
    own, far_a, far_b, far_c, gain, wk_far, wv_far, query, bias_a, bias_b, back_four, back_far, gate,
    pay_ref, expo_ref, dprobs_ref, stat_ref,
    normed, wk, wv, dctx, acc, ksem, vsem,
):
    key_copies = fetch(wk_far, wk, ksem)
    for later in (query, bias_a, bias_b):
        later.start()
    value_copies = fetch(wv_far, wv, vsem)
    for later in (back_four, back_far, gate):
        later.start()
    blocks = [piece.ready() for piece in (own, far_a, far_b, far_c)]
    n_sub, rows, block = blocks[0].shape
    queries, heads, keys = expo_ref.shape
    width = normed.shape[1]
    n_col = width // block
    me = lax.axis_index("row")
    col = lax.axis_index("col")

    def token_block(k, core):
        there = place(k, col, core)
        hop = (me // n_sub + 4 - there // n_sub) % 4
        spot = (me % n_sub) ^ (there % n_sub)
        some = [piece[spot] for piece in blocks]
        return jnp.where(
            hop < 2, jnp.where(hop == 0, some[0], some[1]), jnp.where(hop == 2, some[2], some[3])
        )

    for t in range(keys // rows):
        joined_norm([token_block(k, t) for k in range(n_col)], normed, t * rows)
    both = gained(normed, gain.ready())
    kh, kl = split(project(both, wk, key_copies))
    half = heads // 2
    mask = head_mask(half, width // 2)[None]
    eye = eye_mask(half)[None]

    def lanes(column):
        return jnp.sum(jnp.where(eye, column.reshape(queries, half, 1), 0.0), axis=1)

    parts = []
    query_ref = query.ready()
    bias_refs = [bias_a.ready(), bias_b.ready()]
    for some, part in halves(heads, width):
        bias = jnp.concatenate([b[:, some] for b in bias_refs], axis=0)
        scores = against(query_ref[:, part], mask, kh[:, part], kl[:, part])
        scores = scores + bias.reshape(queries * half, keys)
        top = jnp.max(scores, axis=-1, keepdims=True)
        expo = jnp.exp(scores - top)
        total = jnp.sum(expo, axis=-1, keepdims=True)
        expo_ref[:, some] = expo.reshape(queries, half, keys)
        stat_ref[:, some] = lanes(top)
        lse = lanes(top + jnp.log(total))
        for k in range(n_col):
            pay_ref[k, :, block + some.start : block + some.stop] = lse
        parts.append(expo * (1.0 / total))
    vh, vl = split(project(both, wv, value_copies))
    backs, gate_ref = [back_four.ready(), back_far.ready()], gate.ready()
    n_x = backs[0].shape[0]
    for k in range(n_col):
        part = slice(k * block, (k + 1) * block)
        spot = (col + n_x - k) % n_x
        near = col // n_x == k // n_x
        dctx[:, part] = jnp.where(near, backs[0][spot], backs[1][spot]) * gate_ref[:, part]
    for (some, part), probs in zip(halves(heads, width), parts):
        high, low = vh[:, part], vl[:, part]
        eh, el = split(probs)
        wide = dg(jnp.concatenate([eh, el], axis=1), jnp.concatenate([high, high], axis=0), NN)
        wide = wide + dg(eh, low, NN)
        wide = jnp.where(mask, wide.reshape(queries, half, width // 2), 0.0)
        acc[:, part] = jnp.sum(wide, axis=1)
        dp = against(dctx[:, part], mask, high, low)
        dprobs_ref[:, some] = dp.reshape(queries, half, keys)
        delta = lanes(jnp.sum(probs * dp, axis=-1, keepdims=True))
        for k in range(n_col):
            pay_ref[k, :, block + heads + some.start : block + heads + some.stop] = delta
    for k in range(n_col):
        pay_ref[k, :, :block] = acc[:, k * block : (k + 1) * block]


def moment_kernel(
    x_far, expo_far, dprobs_far, rs_a, rs_b, out_far, x_ref, expo_ref, dprobs_ref, out_ref, sems
):
    heads = expo_ref.shape[1]
    chans = out_ref.shape[2]
    take = [
        Stream(x_far, x_ref, sems.at[0]),
        Stream(expo_far, expo_ref, sems.at[1], 1),
        Stream(dprobs_far, dprobs_ref, sems.at[2], 1),
    ]
    give = Stream(out_ref, out_far, sems.at[3])
    for t in reversed(take):
        t.start()
    for t in take[1:]:
        t.wait()
    cut = PARTS * LARGE // expo_ref.shape[0]

    def step(rs_ref, shift, k, carry):
        take[0].copy(k).wait()
        for j in range(take[0].rows):
            i = k * take[0].rows + j
            e = expo_ref[i] * rs_ref[pl.ds(i - shift, 1), :]
            bh, bl = split(jnp.concatenate([e * dprobs_ref[i], e], axis=0))
            d2 = jnp.concatenate(split(centred(x_ref[i])), axis=1)
            wide = dg(jnp.concatenate([bh, bl], axis=0), d2, NN)
            high = wide[: 2 * heads]
            out_ref[i] = high[:, :chans] + high[:, chans:] + wide[2 * heads :, :chans]
        return carry

    lax.fori_loop(0, cut, functools.partial(step, rs_a.ready(), 0), 0)
    for k in range(cut):
        give.copy(k).start()
    lax.fori_loop(cut, PARTS, functools.partial(step, rs_b.ready(), LARGE), 0)
    for k in range(cut, PARTS):
        give.copy(k).start()
    give.wait()


def packed(x):
    rows, block = x.shape
    half, rest = rows // 2, LANES - block
    low = x[half:]
    right = jnp.concatenate([low[: half // 2, rest:], low[half // 2 :, rest:]], axis=1)
    return jnp.concatenate([jnp.concatenate([x[:half], low[:, :rest]], axis=1), right], axis=0)


def unpacked(x, rows, block):
    half, wide = rows // 2, 2 * block - LANES
    top, low = x[:half], x[half:]
    left = top[:, block:]
    lower = [
        jnp.concatenate([left[: half // 2], low[:, :wide]], axis=1),
        jnp.concatenate([left[half // 2 :], low[:, wide:]], axis=1),
    ]
    return jnp.concatenate([top[:, :block]] + lower, axis=0)


def join_kernel(recv_ref, stat_ref, moment_ref, pgain_ref, pay_ref, join_ref):
    n, rows, lanes = recv_ref.shape
    heads = moment_ref.shape[1] // 2
    block = lanes - 2 * heads
    size = n * block // heads
    lane = lax.broadcasted_iota(jnp.int32, (heads, block), 1) + lax.axis_index("col") * block
    row = lax.broadcasted_iota(jnp.int32, (heads, block), 0) * size
    sel = jnp.where((lane >= row) & (lane < row + size), 1.0, 0.0)
    lse = [recv_ref[k, :, block : block + heads] for k in range(n)]
    top = functools.reduce(jnp.maximum, lse)
    weight = [jnp.exp(v - top) for v in lse]
    total = sum(weight)
    inv = 1.0 / total
    weight = [w * inv for w in weight]
    delta = sum(w * recv_ref[k, :, block + heads :] for k, w in enumerate(weight))
    fac = jnp.exp(stat_ref[:, :heads] - (top + jnp.log(total)))
    join_ref[:, :heads] = fac
    join_ref[:, heads : 2 * heads] = delta
    context = sum(
        lax.dot_general(w, sel, NN, precision=lax.Precision.HIGHEST, preferred_element_type=F32)
        * recv_ref[k, :, :block]
        for k, w in enumerate(weight)
    )
    eye = eye_mask(heads)[None]

    def column(v):
        return jnp.sum(jnp.where(eye, v[:, None, :], 0.0), axis=-1, keepdims=True)

    part = jnp.sum(
        column(fac) * moment_ref[:, :heads] - column(fac * delta) * moment_ref[:, heads:], axis=0
    ) * pgain_ref[...]
    whole = jnp.concatenate([packed(context), part], axis=0)
    for k in range(n):
        pay_ref[k] = whole


def grad_kernel(
    part, x_far, expo_far, dprobs_far, bias_far, rs, joined, wb, pgain, *refs
):
    if part == 0:
        out_far, x_ref, expo_ref, dprobs_ref, bias_ref, fac_ref, dlt_ref, out_ref, sems = refs
    else:
        _, recv, gate, wout, out_far, att_ref = refs[:6]
        x_ref, expo_ref, dprobs_ref, bias_ref, fac_ref, dlt_ref, out_ref, sems, gated = refs[6:]
    count, keys = out_ref.shape[:2]
    shift = part * LARGE
    parts = PARTS // 2
    take = [
        Stream(x_far, x_ref, sems.at[0], parts, shift),
        Stream(expo_far, expo_ref, sems.at[1], 1, shift),
        Stream(dprobs_far, dprobs_ref, sems.at[2], 1, shift),
        Stream(bias_far, bias_ref, sems.at[3], 1),
    ]
    give = Stream(out_ref, out_far, sems.at[4], parts, shift)
    for t in reversed(take):
        t.start()
    heads = expo_ref.shape[1]
    chans = out_ref.shape[2]
    eye = eye_mask(heads)
    wt = centred(wb.ready()[...] * pgain.ready()[...])
    join_ref = joined.ready()
    rs_ref = rs.ready()
    zero = jnp.zeros_like(wt)
    mean = jnp.full_like(wt, 1.0 / chans)
    wh, wl = split(
        jnp.concatenate(
            [jnp.concatenate([wt, zero], axis=1), jnp.concatenate([zero, mean], axis=1)], axis=0
        )
    )

    def spread(w):
        nil = jnp.zeros_like(w)
        rows = [
            jnp.concatenate([w if m == n else nil for n in range(GROUP)], axis=1)
            for m in range(GROUP)
        ]
        return jnp.concatenate(rows, axis=0)

    weights = jnp.concatenate([spread(wh), spread(wh)], axis=0)
    rest = spread(wl)
    mask = eye[None]

    def columns(first):
        value = join_ref[pl.ds(shift, count), first : first + heads]
        value = jnp.where(mask, value[:, None, :], 0.0).reshape(count * heads, heads)
        high, rest = split(value)
        low, least = split(value - high.astype(F32))
        ones = jnp.ones((3 * heads, keys), BF16)
        return dg(jnp.concatenate([high, low, least], axis=1), ones, NN).reshape(count, heads, keys)

    fac_ref[...] = columns(0)
    dlt_ref[...] = columns(heads)
    for t in take[1:]:
        t.wait()

    def cells(i):
        rs = rs_ref[pl.ds(i, 1), :]
        u = expo_ref[i] * fac_ref[i] * (dprobs_ref[i] - dlt_ref[i]) * rs
        return [u, u * bias_ref[i] * rs]

    def step(k, carry):
        take[0].copy(k).wait()
        for j in range(0, give.rows, GROUP):
            first = k * give.rows + j
            rows = [part for m in range(GROUP) for part in cells(first + m)]
            high, low = split(jnp.concatenate(rows, axis=0).T)
            wide = dg(jnp.concatenate([high, low], axis=1), weights, NN) + dg(high, rest, NN)
            for m in range(GROUP):
                one = wide[:, 2 * chans * m : 2 * chans * (m + 1)]
                i = first + m
                out_ref[i] = one[:, :chans] - centred(x_ref[i]) * one[:, chans:]
        give.copy(k).start()
        return carry

    lax.fori_loop(0, parts, step, 0)
    if part == 1:
        attended_rows(recv.ready(), gate.ready(), wout.ready(), att_ref, gated)
    give.wait()


def share_kernel(recv_ref, pay_ref):
    heads = pay_ref.shape[1]
    rows = recv_ref.shape[1] - heads
    total = recv_ref[0, rows:, :]
    for k in range(1, recv_ref.shape[0]):
        total = total + recv_ref[k, rows:, :]
    for k in range(pay_ref.shape[0]):
        pay_ref[k] = total


def attended_rows(recv_ref, gate_ref, wout_ref, att_ref, gated):
    rows, block = att_ref.shape
    for k in range(recv_ref.shape[0]):
        part = slice(k * block, (k + 1) * block)
        held = recv_ref[k, : rows * block // LANES]
        gated[:, part] = unpacked(held, rows, block) * gate_ref[:, part]
    att_ref[...] = dot3(gated[...], wout_ref[...], NT)


def last_kernel(recv_ref, out_ref):
    total = recv_ref[0]
    for k in range(1, recv_ref.shape[0]):
        total = total + recv_ref[k]
    out_ref[...] = total


def place(col, owner, core):
    high, x = col // 4, col % 4
    y, low = owner // 2, owner % 2
    spot = (y + 6 - x + owner % 4) % 4
    near = lax.select(high == owner // 4, low, 1 - low) if not isinstance(owner, int) else (
        low if high == owner // 4 else 1 - low
    )
    return (spot * 2 + near) * 2 + core


def swap(x, axis):
    return lax.all_to_all(x, axis, 0, 0, tiled=True)


def local(
    single, pair, single_gain, pair_gain, w_query, w_key, w_value, w_gate, w_bias, w_out, cotangent
):
    n_row, n_col = lax.axis_size("row"), lax.axis_size("col")
    queries, keys, chans = pair.shape
    heads = w_bias.shape[1]
    width = single_gain.shape[0]
    block = single.shape[1]
    per = n_row // n_col
    gain = single_gain.reshape(-1, chans)
    pgain = pair_gain[None]
    wb = w_bias.T
    wout = w_out.T
    dma = pltpu.SemaphoreType.DMA
    shape_e = sds(queries, heads, keys)

    def mem(shape):
        return pltpu.VMEM(shape.shape, shape.dtype)

    perm = [
        (r * n_col + c, place(c, r // per, r % per) * n_col + r // per)
        for r in range(n_row)
        for c in range(n_col)
    ]
    moved = lax.ppermute(single, ("row", "col"), perm)
    pay1 = call(
        first_kernel,
        sds(n_col, queries + queries // 2, chans),
        2 * queries * width * block * 3,
        (single, cotangent, wout),
    )
    recv1 = swap(pay1, "col")
    shape_x = sds(queries, keys, chans)
    counts = (LARGE, queries - LARGE)
    parts_e = [sds(n, heads, keys) for n in counts]
    parts_rs = [sds(n, keys) for n in counts]
    parts_x = [sds(n, keys, chans) for n in counts]
    held = [
        [mem(x), mem(e), mem(rs), dma((3, PARTS // 2))]
        for x, e, rs in zip(parts_x, parts_e, parts_rs)
    ]
    bias_a, rs_a = call(
        pair_kernel,
        (parts_e[0], parts_rs[0]),
        queries * keys * chans * 200,
        (pair, wb, pgain),
        held[0],
        (0, 1, 1),
        (1, 1),
    )
    moved, rs_a = lax.optimization_barrier((moved, rs_a))

    def along(x, target):
        return lax.ppermute(x, "row", [(r, target(r)) for r in range(n_row)])

    pair_of = jnp.stack([moved, along(moved, lambda r: r ^ 1)])
    back_pay = call(back_kernel, sds(queries, block), queries * width, (recv1,), vmem=4 * MIB)
    four = jnp.concatenate([pair_of, along(pair_of, lambda r: r ^ 2)])
    n_x = 4

    def around(x, k):
        return lax.ppermute(x, "col", [(c, c - c % n_x + (c + k) % n_x) for c in range(n_col)])

    back_four = jnp.stack([back_pay] + [around(back_pay, k) for k in range(1, n_x)])
    back_far = lax.ppermute(back_four, "col", [(c, (c + n_x) % n_col) for c in range(n_col)])
    ring = [along(four, lambda r: (r + 4 * k) % n_row) for k in range(1, 4)]
    recv1, four = lax.optimization_barrier((recv1, four))
    square = pltpu.VMEM((width, width), F32)
    bias_b, rs_b, query, gate = call(
        query_kernel,
        (
            parts_e[1],
            parts_rs[1],
            sds(queries, width),
            sds(queries, width),
        ),
        queries * keys * chans * 200 + queries * width * width * 12,
        (pair, wb, pgain, recv1, gain, w_query, w_gate),
        held[1] + [pltpu.VMEM((queries, width), F32), square, square, dma((3,)), dma((3,))],
        (0, 1, 1, 1, 1, 0, 0),
        (1, 1, 0, 0),
    )
    pay4, expo, dprobs, stat = call(
        attend_kernel,
        (sds(n_col, queries, chans), shape_e, shape_e, sds(queries, chans)),
        keys * width * width * 12,
        (four, *ring, gain, w_key, w_value, query, bias_a, bias_b, back_four, back_far, gate),
        [
            pltpu.VMEM((keys, width), F32),
            square,
            square,
            pltpu.VMEM((queries, width), F32),
            pltpu.VMEM((queries, width), F32),
            dma((3,)),
            dma((3,)),
        ],
        (1, 1, 1, 1, 1, 0, 0, 2, 2, 2, 2, 2, 2),
    )
    recv4 = swap(pay4, "col")
    shape_m = sds(queries, 2 * heads, chans)
    moment = call(
        moment_kernel,
        shape_m,
        queries * keys * chans * heads * 12,
        (pair, expo, dprobs, rs_a, rs_b),
        [mem(shape_x), mem(shape_e), mem(shape_e), mem(shape_m), dma((4, PARTS))],
        (0, 0, 0, 1, 1),
        (1,),
    )
    pay5, joined = call(
        join_kernel,
        (sds(n_col, queries * block // LANES + heads, chans), sds(queries, chans)),
        queries * heads * chans * 8,
        (recv4, stat, moment, pgain),
    )
    recv5 = swap(pay5, "col")
    cost = queries * keys * chans * 200
    held = [
        [mem(x)] + 5 * [mem(e)] + [mem(x), dma((5, PARTS // 2))] for x, e in zip(parts_x, parts_e)
    ]
    place_of = (0, 0, 0, 0, 1, 1, 1, 1)
    first = call(
        functools.partial(grad_kernel, 0),
        shape_x,
        cost,
        (pair, expo, dprobs, bias_a, rs_a, joined, wb, pgain),
        held[0],
        place_of,
        (1,),
    )
    recv5, first = lax.optimization_barrier((recv5, first))
    pay6 = call(
        share_kernel, sds(n_row, heads, chans), queries * width, (recv5,), vmem=4 * MIB
    )
    recv6 = swap(pay6, "row")
    pair_grad, attended = call(
        functools.partial(grad_kernel, 1),
        (shape_x, sds(queries, block)),
        cost,
        (pair, expo, dprobs, bias_b, rs_b, joined, wb, pgain, first, recv5, gate, wout),
        held[1] + [pltpu.VMEM((queries, width), F32)],
        place_of + (0, 1, 1, 1),
        (1, 0),
        {8: 0},
    )
    recv6, pair_grad, attended = lax.optimization_barrier((recv6, pair_grad, attended))
    bias_grad = call(last_kernel, sds(heads, chans), chans * heads, (recv6,), vmem=4 * MIB)
    return attended, pair_grad, bias_grad.T


def solution(mesh):
    placed = (
        P("row", "col"),
        P("row", "col", None),
        P(),
        P(),
        P(),
        P(),
        P(),
        P(),
        P(),
        P(None, "col"),
        P("row", "col"),
    )
    return jax.shard_map(
        local,
        mesh=mesh,
        in_specs=placed,
        out_specs=(P("row", "col"), P("row", "col", None), P()),
        check_vma=False,
    )
```

```python
import functools

import jax
import jax.numpy as jnp
from jax import lax
from jax.experimental import pallas as pl
from jax.experimental.pallas import tpu as pltpu
from jax.sharding import PartitionSpec as P

F32 = jnp.float32
BF16 = jnp.bfloat16
EPS = 1e-05
NN = (((1,), (0,)), ((), ()))
NT = (((1,), (1,)), ((), ()))
TN = (((0,), (0,)), ((), ()))
MIB = 1024 * 1024
VMEM_BYTES = 60 * MIB
PARTS = 4
GROUP = 4
LANES = 128
LARGE = 48
FAR = pl.BlockSpec(memory_space=pl.ANY)
NEAR = pl.BlockSpec(memory_space=pltpu.VMEM)


def split(x):
    high = x.astype(BF16)
    return high, (x - high.astype(F32)).astype(BF16)


def dg(a, b, dims):
    return lax.dot_general(a, b, dims, preferred_element_type=F32)


def dot3(a, b, dims):
    ah, al = split(a)
    bh, bl = split(b)
    return dg(ah, bh, dims) + dg(al, bh, dims) + dg(ah, bl, dims)


class Near:
    def __init__(self, src, dst, sem):
        self.copy = pltpu.make_async_copy(src, dst, sem)
        self.dst = dst
        self.waiting = True

    def start(self):
        self.copy.start()
        return self

    def ready(self):
        if self.waiting:
            self.copy.wait()
            self.waiting = False
        return self.dst


def call(kernel, out_shape, flops, args, scratch=(), near=None, far_out=None, alias=None, vmem=VMEM_BYTES):
    nbytes = sum(a.size * a.dtype.itemsize for a in args)
    for o in jax.tree.leaves(out_shape):
        nbytes += o.size * jnp.dtype(o.dtype).itemsize
    kw = {} if alias is None else {"input_output_aliases": alias}
    scratch = list(scratch)
    body = kernel
    if near is not None:
        kw["in_specs"] = [FAR] * len(args)
        small = [k for k, yes in enumerate(near) if yes]
        scratch += [pltpu.VMEM(args[k].shape, args[k].dtype) for k in small]
        scratch.append(pltpu.SemaphoreType.DMA((len(small),)))

        def body(*refs):
            refs = list(refs)
            places = refs[-len(small) - 1 : -1]
            for n, (k, place_) in enumerate(zip(small, places)):
                refs[k] = Near(refs[k], place_, refs[-1].at[n])
                if near[k] == 1:
                    refs[k].start()
            kernel(*refs[: -len(small) - 1])

    if far_out is not None:
        specs = tuple(FAR if far else NEAR for far in far_out)
        kw["out_specs"] = specs if isinstance(out_shape, tuple) else specs[0]
    return pl.pallas_call(
        body,
        out_shape=out_shape,
        scratch_shapes=scratch,
        compiler_params=pltpu.CompilerParams(vmem_limit_bytes=vmem),
        cost_estimate=pl.CostEstimate(flops=flops, bytes_accessed=nbytes, transcendentals=0),
        **kw,
    )(*args)


class Stream:
    def __init__(self, src, dst, sems, parts=PARTS, shift=0):
        self.src, self.dst, self.sems, self.parts = src, dst, sems, parts
        self.rows = min(src.shape[0], dst.shape[0]) // parts
        self.src_shift = shift if src.shape[0] > dst.shape[0] else 0
        self.dst_shift = shift if src.shape[0] < dst.shape[0] else 0

    def copy(self, k):
        first = pl.multiple_of(k * self.rows, self.rows)
        there = pl.ds(first + self.src_shift, self.rows)
        here = pl.ds(first + self.dst_shift, self.rows)
        return pltpu.make_async_copy(self.src.at[there], self.dst.at[here], self.sems.at[k])

    def start(self):
        for k in range(self.parts):
            self.copy(k).start()

    def wait(self):
        for k in range(self.parts):
            self.copy(k).wait()


def sds(*shape, dtype=F32):
    return jax.ShapeDtypeStruct(shape, dtype)


def head_mask(heads, width):
    lane = lax.broadcasted_iota(jnp.int32, (heads, width), 1)
    row = lax.broadcasted_iota(jnp.int32, (heads, width), 0)
    size = width // heads
    return (lane >= row * size) & (lane < (row + 1) * size)


def eye_mask(n):
    return lax.broadcasted_iota(jnp.int32, (n, n), 0) == lax.broadcasted_iota(jnp.int32, (n, n), 1)


def packed(x):
    rows, block = x.shape
    half, rest = rows // 2, LANES - block
    low = x[half:]
    right = jnp.concatenate([low[: half // 2, rest:], low[half // 2 :, rest:]], axis=1)
    return jnp.concatenate([jnp.concatenate([x[:half], low[:, :rest]], axis=1), right], axis=0)


def unpacked(x, rows, block):
    half, wide = rows // 2, 2 * block - LANES
    top, low = x[:half], x[half:]
    left = top[:, block:]
    lower = [
        jnp.concatenate([left[: half // 2], low[:, :wide]], axis=1),
        jnp.concatenate([left[half // 2 :], low[:, wide:]], axis=1),
    ]
    return jnp.concatenate([top[:, :block]] + lower, axis=0)


def first_kernel(single_ref, cot_ref, wout_ref, out_ref, packed_ref):
    packed_ref[...] = packed(single_ref[...])
    n, _, lanes = out_ref.shape
    rows, block = single_ref.shape
    rest = lanes - block
    half = rows // 2
    single = single_ref[...]
    ch, cl = split(cot_ref[...])
    wh, wl = split(wout_ref[...])
    two = dg(jnp.concatenate([ch, cl], axis=0), wh, NN)
    full = two[:rows] + two[rows:] + dg(ch, wl, NN)
    for k in range(n):
        part = full[:, k * block : (k + 1) * block]
        out_ref[k, :rows, :block] = single
        out_ref[k, :rows, block:] = part[:, :rest]
        out_ref[k, rows:, : block - rest] = part[:half, rest:]
        out_ref[k, rows:, block - rest :] = part[half:, rest:]


def joined_norm(blocks, out_ref, row):
    rows, block = blocks[0].shape
    width = block * len(blocks)
    centre = sum(jnp.sum(b, axis=-1, keepdims=True) for b in blocks) / width
    blocks = [b - centre for b in blocks]
    spread = sum(jnp.sum(b * b, axis=-1, keepdims=True) for b in blocks) / width
    scale = lax.rsqrt(spread + EPS)
    for k, b in enumerate(blocks):
        part = slice(k * block, (k + 1) * block)
        out_ref[row : row + rows, part] = b * scale


def gained(normed, gain_ref):
    tiles, lanes = gain_ref.shape
    parts = [
        split(normed[:, t * lanes : (t + 1) * lanes] * gain_ref[t : t + 1, :]) for t in range(tiles)
    ]
    return jnp.concatenate(
        [jnp.concatenate([p[k] for p in parts], axis=1) for k in range(2)], axis=0
    )


def project(both, weight, copies):
    rows = both.shape[0] // 2
    third = weight.shape[0] // 3
    out = None
    for k, one in enumerate(copies):
        one.wait()
        here = slice(k * third, (k + 1) * third)
        wh, wl = split(weight[here, :])
        two = dg(both[:, here], wh, NN)
        part = two[:rows] + two[rows:] + dg(both[:rows, here], wl, NN)
        out = part if out is None else out + part
    return out


def fetch(src, dst, sems):
    rows = src.shape[0] // 3
    out = []
    for k in range(3):
        here = pl.ds(k * rows, rows)
        one = pltpu.make_async_copy(src.at[here], dst.at[here], sems.at[k])
        one.start()
        out.append(one)
    return out


def back_kernel(recv_ref, back_ref):
    rows, block = back_ref.shape
    total = recv_ref[0]
    for k in range(1, recv_ref.shape[0]):
        total = total + recv_ref[k]
    rest = total.shape[1] - block
    right = jnp.concatenate([total[rows:, : block - rest], total[rows:, block - rest :]], axis=0)
    total = jnp.concatenate([total[:rows, block:], right], axis=1)
    back_ref[...] = total


def query_kernel(
    pair_far, wb, pgain, recv, gain, wq_far, wg_far,
    bias_far, rs_far, query_ref, gate_ref,
    x_ref, bias_ref, rs_ref, sems, normed, wq, wg, qsem, gsem,
):
    take, give = bias_streams(pair_far, bias_far, rs_far, x_ref, bias_ref, rs_ref, sems, 1)
    query_copies = fetch(wq_far, wq, qsem)
    gate_copies = fetch(wg_far, wg, gsem)
    bias_rows(take, give, wb.ready(), pgain.ready(), x_ref, bias_ref, rs_ref)
    recv_ref = recv.ready()
    n = recv_ref.shape[0]
    rows, width = query_ref.shape
    joined_norm([recv_ref[k, :rows, : width // n] for k in range(n)], normed, 0)
    both = gained(normed, gain.ready())
    query_ref[...] = project(both, wq, query_copies) * (48 ** -0.5)
    gate_ref[...] = 1.0 / (1.0 + jnp.exp(-project(both, wg, gate_copies)))
    for g in give:
        g.wait()


def centred(x):
    return x - jnp.sum(x, axis=-1, keepdims=True) * (1.0 / x.shape[-1])


def bias_streams(pair_far, bias_far, rs_far, x_ref, bias_ref, rs_ref, sems, part):
    parts = PARTS // 2
    take = Stream(pair_far, x_ref, sems.at[0], parts, part * LARGE)
    take.start()
    return take, [Stream(bias_ref, bias_far, sems.at[1], 1), Stream(rs_ref, rs_far, sems.at[2], 1)]


def bias_rows(take, give, wb_ref, pgain_ref, x_ref, bias_ref, rs_ref):
    chans = x_ref.shape[2]
    heads = bias_ref.shape[1]
    wh, wl = split(wb_ref[...] * pgain_ref[...])
    top = jnp.concatenate([wh, wh], axis=1)
    left = jnp.concatenate([top, jnp.concatenate([wl, jnp.zeros_like(wl)], axis=1)], axis=0)
    ones = jnp.ones((8, 2 * chans), BF16)

    def step(k, carry):
        take.copy(k).wait()
        for j in range(take.rows):
            i = k * take.rows + j
            d = centred(x_ref[i])
            spread = dg(ones, jnp.concatenate(split(d * d), axis=1), NT) * (1.0 / chans)
            rs = lax.rsqrt(spread[0:1] + EPS)
            two = dg(left, jnp.concatenate(split(d), axis=1), NT)
            bias_ref[i] = (two[:heads] + two[heads:]) * rs
            rs_ref[pl.ds(i, 1), :] = rs
        return carry

    lax.fori_loop(0, take.parts, step, 0)
    for g in give:
        g.start()


def pair_kernel(pair_far, wb, pgain, bias_far, rs_far, x_ref, bias_ref, rs_ref, sems):
    take, give = bias_streams(pair_far, bias_far, rs_far, x_ref, bias_ref, rs_ref, sems, 0)
    bias_rows(take, give, wb.ready(), pgain.ready(), x_ref, bias_ref, rs_ref)
    for g in give:
        g.wait()


def halves(heads, width):
    return [
        (slice(g * heads // 2, (g + 1) * heads // 2), slice(g * width // 2, (g + 1) * width // 2))
        for g in range(2)
    ]


def by_head(rows, mask):
    wide = jnp.where(mask, rows[:, None, :], 0.0)
    return split(wide.reshape(-1, rows.shape[1]))


def against(rows, mask, high, low):
    keys = high.shape[0]
    rh, rl = by_head(rows, mask)
    two = dg(rh, jnp.concatenate([high, low], axis=0), NT)
    return two[:, :keys] + two[:, keys:] + dg(rl, high, NT)


def attend_kernel(
    own, far_a, far_b, far_c, gain, wk_far, wv_far, query, bias_a, bias_b, back_four, back_far, gate,
    pay_ref, expo_ref, dprobs_ref, stat_ref,
    normed, wk, wv, dctx, acc, ksem, vsem,
):
    key_copies = fetch(wk_far, wk, ksem)
    for later in (query, bias_a, bias_b):
        later.start()
    value_copies = fetch(wv_far, wv, vsem)
    for later in (back_four, back_far, gate):
        later.start()
    blocks = [piece.ready() for piece in (own, far_a, far_b, far_c)]
    n_sub = blocks[0].shape[0]
    rows, block = back_four.dst.shape[1:]
    queries, heads, keys = expo_ref.shape
    width = normed.shape[1]
    n_col = width // block
    me = lax.axis_index("row")
    col = lax.axis_index("col")

    def token_block(k, core):
        there = place(k, col, core)
        hop = (me // n_sub + 4 - there // n_sub) % 4
        spot = (me % n_sub) ^ (there % n_sub)
        some = [piece[spot] for piece in blocks]
        one = jnp.where(
            hop < 2, jnp.where(hop == 0, some[0], some[1]), jnp.where(hop == 2, some[2], some[3])
        )
        return unpacked(one, rows, block)

    for t in range(keys // rows):
        joined_norm([token_block(k, t) for k in range(n_col)], normed, t * rows)
    both = gained(normed, gain.ready())
    kh, kl = split(project(both, wk, key_copies))
    half = heads // 2
    mask = head_mask(half, width // 2)[None]
    eye = eye_mask(half)[None]

    def lanes(column):
        return jnp.sum(jnp.where(eye, column.reshape(queries, half, 1), 0.0), axis=1)

    parts = []
    query_ref = query.ready()
    bias_refs = [bias_a.ready(), bias_b.ready()]
    for some, part in halves(heads, width):
        bias = jnp.concatenate([b[:, some] for b in bias_refs], axis=0)
        scores = against(query_ref[:, part], mask, kh[:, part], kl[:, part])
        scores = scores + bias.reshape(queries * half, keys)
        top = jnp.max(scores, axis=-1, keepdims=True)
        expo = jnp.exp(scores - top)
        total = jnp.sum(expo, axis=-1, keepdims=True)
        expo_ref[:, some] = expo.reshape(queries, half, keys)
        stat_ref[:, some] = lanes(top)
        lse = lanes(top + jnp.log(total))
        for k in range(n_col):
            pay_ref[k, :, block + some.start : block + some.stop] = lse
        parts.append(expo * (1.0 / total))
    vh, vl = split(project(both, wv, value_copies))
    backs, gate_ref = [back_four.ready(), back_far.ready()], gate.ready()
    n_x = backs[0].shape[0]
    for k in range(n_col):
        part = slice(k * block, (k + 1) * block)
        spot = (col + n_x - k) % n_x
        near = col // n_x == k // n_x
        dctx[:, part] = jnp.where(near, backs[0][spot], backs[1][spot]) * gate_ref[:, part]
    for (some, part), probs in zip(halves(heads, width), parts):
        high, low = vh[:, part], vl[:, part]
        eh, el = split(probs)
        wide = dg(jnp.concatenate([eh, el], axis=1), jnp.concatenate([high, high], axis=0), NN)
        wide = wide + dg(eh, low, NN)
        wide = jnp.where(mask, wide.reshape(queries, half, width // 2), 0.0)
        acc[:, part] = jnp.sum(wide, axis=1)
        dp = against(dctx[:, part], mask, high, low)
        dprobs_ref[:, some] = dp.reshape(queries, half, keys)
        delta = lanes(jnp.sum(probs * dp, axis=-1, keepdims=True))
        for k in range(n_col):
            pay_ref[k, :, block + heads + some.start : block + heads + some.stop] = delta
    for k in range(n_col):
        pay_ref[k, :, :block] = acc[:, k * block : (k + 1) * block]


def moment_kernel(
    x_far, expo_far, dprobs_far, rs_a, rs_b, out_far, x_ref, expo_ref, dprobs_ref, out_ref, sems
):
    heads = expo_ref.shape[1]
    chans = out_ref.shape[2]
    take = [
        Stream(x_far, x_ref, sems.at[0]),
        Stream(expo_far, expo_ref, sems.at[1], 1),
        Stream(dprobs_far, dprobs_ref, sems.at[2], 1),
    ]
    give = Stream(out_ref, out_far, sems.at[3])
    for t in reversed(take):
        t.start()
    for t in take[1:]:
        t.wait()
    cut = PARTS * LARGE // expo_ref.shape[0]

    def step(rs_ref, shift, k, carry):
        take[0].copy(k).wait()
        for j in range(take[0].rows):
            i = k * take[0].rows + j
            e = expo_ref[i] * rs_ref[pl.ds(i - shift, 1), :]
            bh, bl = split(jnp.concatenate([e * dprobs_ref[i], e], axis=0))
            d2 = jnp.concatenate(split(centred(x_ref[i])), axis=1)
            wide = dg(jnp.concatenate([bh, bl], axis=0), d2, NN)
            high = wide[: 2 * heads]
            out_ref[i] = high[:, :chans] + high[:, chans:] + wide[2 * heads :, :chans]
        return carry

    lax.fori_loop(0, cut, functools.partial(step, rs_a.ready(), 0), 0)
    for k in range(cut):
        give.copy(k).start()
    lax.fori_loop(cut, PARTS, functools.partial(step, rs_b.ready(), LARGE), 0)
    for k in range(cut, PARTS):
        give.copy(k).start()
    give.wait()


def join_kernel(recv_ref, stat_ref, moment_ref, pgain_ref, pay_ref, join_ref):
    n, rows, lanes = recv_ref.shape
    heads = moment_ref.shape[1] // 2
    block = lanes - 2 * heads
    size = n * block // heads
    lane = lax.broadcasted_iota(jnp.int32, (heads, block), 1) + lax.axis_index("col") * block
    row = lax.broadcasted_iota(jnp.int32, (heads, block), 0) * size
    sel = jnp.where((lane >= row) & (lane < row + size), 1.0, 0.0)
    lse = [recv_ref[k, :, block : block + heads] for k in range(n)]
    top = functools.reduce(jnp.maximum, lse)
    weight = [jnp.exp(v - top) for v in lse]
    total = sum(weight)
    inv = 1.0 / total
    weight = [w * inv for w in weight]
    delta = sum(w * recv_ref[k, :, block + heads :] for k, w in enumerate(weight))
    fac = jnp.exp(stat_ref[:, :heads] - (top + jnp.log(total)))
    join_ref[:, :heads] = fac
    join_ref[:, heads : 2 * heads] = delta
    context = sum(
        lax.dot_general(w, sel, NN, precision=lax.Precision.HIGHEST, preferred_element_type=F32)
        * recv_ref[k, :, :block]
        for k, w in enumerate(weight)
    )
    eye = eye_mask(heads)[None]

    def column(v):
        return jnp.sum(jnp.where(eye, v[:, None, :], 0.0), axis=-1, keepdims=True)

    part = jnp.sum(
        column(fac) * moment_ref[:, :heads] - column(fac * delta) * moment_ref[:, heads:], axis=0
    ) * pgain_ref[...]
    whole = jnp.concatenate([packed(context), part], axis=0)
    for k in range(n):
        pay_ref[k] = whole


def grad_kernel(
    part, x_far, expo_far, dprobs_far, bias_far, rs, joined, wb, pgain, *refs
):
    if part == 0:
        out_far, x_ref, expo_ref, dprobs_ref, bias_ref, fac_ref, dlt_ref, out_ref, sems = refs
    else:
        _, recv, gate, wout, out_far, att_ref = refs[:6]
        x_ref, expo_ref, dprobs_ref, bias_ref, fac_ref, dlt_ref, out_ref, sems, gated = refs[6:]
    count, keys = out_ref.shape[:2]
    shift = part * LARGE
    parts = PARTS // 2
    take = [
        Stream(x_far, x_ref, sems.at[0], parts, shift),
        Stream(expo_far, expo_ref, sems.at[1], 1, shift),
        Stream(dprobs_far, dprobs_ref, sems.at[2], 1, shift),
        Stream(bias_far, bias_ref, sems.at[3], 1),
    ]
    give = Stream(out_ref, out_far, sems.at[4], parts, shift)
    for t in reversed(take):
        t.start()
    heads = expo_ref.shape[1]
    chans = out_ref.shape[2]
    eye = eye_mask(heads)
    wt = centred(wb.ready()[...] * pgain.ready()[...])
    join_ref = joined.ready()
    rs_ref = rs.ready()
    zero = jnp.zeros_like(wt)
    mean = jnp.full_like(wt, 1.0 / chans)
    wh, wl = split(
        jnp.concatenate(
            [jnp.concatenate([wt, zero], axis=1), jnp.concatenate([zero, mean], axis=1)], axis=0
        )
    )

    def spread(w):
        nil = jnp.zeros_like(w)
        rows = [
            jnp.concatenate([w if m == n else nil for n in range(GROUP)], axis=1)
            for m in range(GROUP)
        ]
        return jnp.concatenate(rows, axis=0)

    weights = jnp.concatenate([spread(wh), spread(wh)], axis=0)
    rest = spread(wl)
    mask = eye[None]

    def columns(first):
        value = join_ref[pl.ds(shift, count), first : first + heads]
        value = jnp.where(mask, value[:, None, :], 0.0).reshape(count * heads, heads)
        high, rest = split(value)
        low, least = split(value - high.astype(F32))
        ones = jnp.ones((3 * heads, keys), BF16)
        return dg(jnp.concatenate([high, low, least], axis=1), ones, NN).reshape(count, heads, keys)

    fac_ref[...] = columns(0)
    dlt_ref[...] = columns(heads)
    for t in take[1:]:
        t.wait()

    def cells(i):
        rs = rs_ref[pl.ds(i, 1), :]
        u = expo_ref[i] * fac_ref[i] * (dprobs_ref[i] - dlt_ref[i]) * rs
        return [u, u * bias_ref[i] * rs]

    def step(k, carry):
        take[0].copy(k).wait()
        for j in range(0, give.rows, GROUP):
            first = k * give.rows + j
            rows = [part for m in range(GROUP) for part in cells(first + m)]
            high, low = split(jnp.concatenate(rows, axis=0).T)
            wide = dg(jnp.concatenate([high, low], axis=1), weights, NN) + dg(high, rest, NN)
            for m in range(GROUP):
                one = wide[:, 2 * chans * m : 2 * chans * (m + 1)]
                i = first + m
                out_ref[i] = one[:, :chans] - centred(x_ref[i]) * one[:, chans:]
        give.copy(k).start()
        return carry

    lax.fori_loop(0, parts, step, 0)
    if part == 1:
        attended_rows(recv.ready(), gate.ready(), wout.ready(), att_ref, gated)
    give.wait()


def share_kernel(recv_ref, pay_ref):
    heads = pay_ref.shape[1]
    rows = recv_ref.shape[1] - heads
    total = recv_ref[0, rows:, :]
    for k in range(1, recv_ref.shape[0]):
        total = total + recv_ref[k, rows:, :]
    for k in range(pay_ref.shape[0]):
        pay_ref[k] = total


def attended_rows(recv_ref, gate_ref, wout_ref, att_ref, gated):
    rows, block = att_ref.shape
    for k in range(recv_ref.shape[0]):
        part = slice(k * block, (k + 1) * block)
        held = recv_ref[k, : rows * block // LANES]
        gated[:, part] = unpacked(held, rows, block) * gate_ref[:, part]
    att_ref[...] = dot3(gated[...], wout_ref[...], NT)


def last_kernel(recv_ref, out_ref):
    total = recv_ref[0]
    for k in range(1, recv_ref.shape[0]):
        total = total + recv_ref[k]
    out_ref[...] = total


def place(col, owner, core):
    high, x = col // 4, col % 4
    y, low = owner // 2, owner % 2
    spot = (y + 6 - x + owner % 4) % 4
    near = lax.select(high == owner // 4, low, 1 - low) if not isinstance(owner, int) else (
        low if high == owner // 4 else 1 - low
    )
    return (spot * 2 + near) * 2 + core


def swap(x, axis):
    return lax.all_to_all(x, axis, 0, 0, tiled=True)


def local(
    single, pair, single_gain, pair_gain, w_query, w_key, w_value, w_gate, w_bias, w_out, cotangent
):
    n_row, n_col = lax.axis_size("row"), lax.axis_size("col")
    queries, keys, chans = pair.shape
    heads = w_bias.shape[1]
    width = single_gain.shape[0]
    block = single.shape[1]
    per = n_row // n_col
    gain = single_gain.reshape(-1, chans)
    pgain = pair_gain[None]
    wb = w_bias.T
    wout = w_out.T
    dma = pltpu.SemaphoreType.DMA
    shape_e = sds(queries, heads, keys)

    def mem(shape):
        return pltpu.VMEM(shape.shape, shape.dtype)

    perm = [
        (r * n_col + c, place(c, r // per, r % per) * n_col + r // per)
        for r in range(n_row)
        for c in range(n_col)
    ]
    pay1, packed_single = call(
        first_kernel,
        (sds(n_col, queries + queries // 2, chans), sds(queries * block // LANES, LANES)),
        2 * queries * width * block * 3,
        (single, cotangent, wout),
    )
    moved = lax.ppermute(packed_single, ("row", "col"), perm)
    recv1 = swap(pay1, "col")
    shape_x = sds(queries, keys, chans)
    counts = (LARGE, queries - LARGE)
    parts_e = [sds(n, heads, keys) for n in counts]
    parts_rs = [sds(n, keys) for n in counts]
    parts_x = [sds(n, keys, chans) for n in counts]
    held = [
        [mem(x), mem(e), mem(rs), dma((3, PARTS // 2))]
        for x, e, rs in zip(parts_x, parts_e, parts_rs)
    ]
    bias_a, rs_a = call(
        pair_kernel,
        (parts_e[0], parts_rs[0]),
        queries * keys * chans * 200,
        (pair, wb, pgain),
        held[0],
        (0, 1, 1),
        (1, 1),
    )
    moved, rs_a = lax.optimization_barrier((moved, rs_a))

    def along(x, target):
        return lax.ppermute(x, "row", [(r, target(r)) for r in range(n_row)])

    pair_of = jnp.stack([moved, along(moved, lambda r: r ^ 1)])
    back_pay = call(back_kernel, sds(queries, block), queries * width, (recv1,), vmem=4 * MIB)
    four = jnp.concatenate([pair_of, along(pair_of, lambda r: r ^ 2)])
    n_x = 4

    def around(x, k):
        return lax.ppermute(x, "col", [(c, c - c % n_x + (c + k) % n_x) for c in range(n_col)])

    back_four = jnp.stack([back_pay] + [around(back_pay, k) for k in range(1, n_x)])
    back_far = lax.ppermute(back_four, "col", [(c, (c + n_x) % n_col) for c in range(n_col)])
    ring = [along(four, lambda r: (r + 4 * k) % n_row) for k in range(1, 4)]
    recv1, four = lax.optimization_barrier((recv1, four))
    square = pltpu.VMEM((width, width), F32)
    bias_b, rs_b, query, gate = call(
        query_kernel,
        (
            parts_e[1],
            parts_rs[1],
            sds(queries, width),
            sds(queries, width),
        ),
        queries * keys * chans * 200 + queries * width * width * 12,
        (pair, wb, pgain, recv1, gain, w_query, w_gate),
        held[1] + [pltpu.VMEM((queries, width), F32), square, square, dma((3,)), dma((3,))],
        (0, 1, 1, 1, 1, 0, 0),
        (1, 1, 0, 0),
    )
    pay4, expo, dprobs, stat = call(
        attend_kernel,
        (sds(n_col, queries, chans), shape_e, shape_e, sds(queries, chans)),
        keys * width * width * 12,
        (four, *ring, gain, w_key, w_value, query, bias_a, bias_b, back_four, back_far, gate),
        [
            pltpu.VMEM((keys, width), F32),
            square,
            square,
            pltpu.VMEM((queries, width), F32),
            pltpu.VMEM((queries, width), F32),
            dma((3,)),
            dma((3,)),
        ],
        (1, 1, 1, 1, 1, 0, 0, 2, 2, 2, 2, 2, 2),
    )
    recv4 = swap(pay4, "col")
    shape_m = sds(queries, 2 * heads, chans)
    moment = call(
        moment_kernel,
        shape_m,
        queries * keys * chans * heads * 12,
        (pair, expo, dprobs, rs_a, rs_b),
        [mem(shape_x), mem(shape_e), mem(shape_e), mem(shape_m), dma((4, PARTS))],
        (0, 0, 0, 1, 1),
        (1,),
    )
    pay5, joined = call(
        join_kernel,
        (sds(n_col, queries * block // LANES + heads, chans), sds(queries, chans)),
        queries * heads * chans * 8,
        (recv4, stat, moment, pgain),
    )
    recv5 = swap(pay5, "col")
    cost = queries * keys * chans * 200
    held = [
        [mem(x)] + 5 * [mem(e)] + [mem(x), dma((5, PARTS // 2))] for x, e in zip(parts_x, parts_e)
    ]
    place_of = (0, 0, 0, 0, 1, 1, 1, 1)
    first = call(
        functools.partial(grad_kernel, 0),
        shape_x,
        cost,
        (pair, expo, dprobs, bias_a, rs_a, joined, wb, pgain),
        held[0],
        place_of,
        (1,),
    )
    recv5, first = lax.optimization_barrier((recv5, first))
    pay6 = call(
        share_kernel, sds(n_row, heads, chans), queries * width, (recv5,), vmem=4 * MIB
    )
    recv6 = swap(pay6, "row")
    pair_grad, attended = call(
        functools.partial(grad_kernel, 1),
        (shape_x, sds(queries, block)),
        cost,
        (pair, expo, dprobs, bias_b, rs_b, joined, wb, pgain, first, recv5, gate, wout),
        held[1] + [pltpu.VMEM((queries, width), F32)],
        place_of + (0, 1, 1, 1),
        (1, 0),
        {8: 0},
    )
    recv6, pair_grad, attended = lax.optimization_barrier((recv6, pair_grad, attended))
    bias_grad = call(last_kernel, sds(heads, chans), chans * heads, (recv6,), vmem=4 * MIB)
    return attended, pair_grad, bias_grad.T


def solution(mesh):
    placed = (
        P("row", "col"),
        P("row", "col", None),
        P(),
        P(),
        P(),
        P(),
        P(),
        P(),
        P(),
        P(None, "col"),
        P("row", "col"),
    )
    return jax.shard_map(
        local,
        mesh=mesh,
        in_specs=placed,
        out_specs=(P("row", "col"), P("row", "col", None), P()),
        check_vma=False,
    )
```

```python
import functools

import jax
import jax.numpy as jnp
from jax import lax
from jax.experimental import pallas as pl
from jax.experimental.pallas import tpu as pltpu
from jax.sharding import PartitionSpec as P

F32 = jnp.float32
BF16 = jnp.bfloat16
EPS = 1e-05
NN = (((1,), (0,)), ((), ()))
NT = (((1,), (1,)), ((), ()))
TN = (((0,), (0,)), ((), ()))
MIB = 1024 * 1024
VMEM_BYTES = 60 * MIB
PARTS = 4
GROUP = 4
LANES = 128
LARGE = 48
FAR = pl.BlockSpec(memory_space=pl.ANY)
NEAR = pl.BlockSpec(memory_space=pltpu.VMEM)


def split(x):
    high = x.astype(BF16)
    return high, (x - high.astype(F32)).astype(BF16)


def dg(a, b, dims):
    return lax.dot_general(a, b, dims, preferred_element_type=F32)


def dot3(a, b, dims):
    ah, al = split(a)
    bh, bl = split(b)
    return dg(ah, bh, dims) + dg(al, bh, dims) + dg(ah, bl, dims)


class Near:
    def __init__(self, src, dst, sem):
        self.copy = pltpu.make_async_copy(src, dst, sem)
        self.dst = dst
        self.waiting = True

    def start(self):
        self.copy.start()
        return self

    def ready(self):
        if self.waiting:
            self.copy.wait()
            self.waiting = False
        return self.dst


def call(kernel, out_shape, flops, args, scratch=(), near=None, far_out=None, alias=None, vmem=VMEM_BYTES):
    nbytes = sum(a.size * a.dtype.itemsize for a in args)
    for o in jax.tree.leaves(out_shape):
        nbytes += o.size * jnp.dtype(o.dtype).itemsize
    kw = {} if alias is None else {"input_output_aliases": alias}
    scratch = list(scratch)
    body = kernel
    if near is not None:
        kw["in_specs"] = [FAR] * len(args)
        small = [k for k, yes in enumerate(near) if yes]
        scratch += [pltpu.VMEM(args[k].shape, args[k].dtype) for k in small]
        scratch.append(pltpu.SemaphoreType.DMA((len(small),)))

        def body(*refs):
            refs = list(refs)
            places = refs[-len(small) - 1 : -1]
            for n, (k, place_) in enumerate(zip(small, places)):
                refs[k] = Near(refs[k], place_, refs[-1].at[n])
                if near[k] == 1:
                    refs[k].start()
            kernel(*refs[: -len(small) - 1])

    if far_out is not None:
        specs = tuple(FAR if far else NEAR for far in far_out)
        kw["out_specs"] = specs if isinstance(out_shape, tuple) else specs[0]
    return pl.pallas_call(
        body,
        out_shape=out_shape,
        scratch_shapes=scratch,
        compiler_params=pltpu.CompilerParams(vmem_limit_bytes=vmem),
        cost_estimate=pl.CostEstimate(flops=flops, bytes_accessed=nbytes, transcendentals=0),
        **kw,
    )(*args)


class Stream:
    def __init__(self, src, dst, sems, parts=PARTS, shift=0):
        self.src, self.dst, self.sems, self.parts = src, dst, sems, parts
        self.rows = min(src.shape[0], dst.shape[0]) // parts
        self.src_shift = shift if src.shape[0] > dst.shape[0] else 0
        self.dst_shift = shift if src.shape[0] < dst.shape[0] else 0

    def copy(self, k):
        first = pl.multiple_of(k * self.rows, self.rows)
        there = pl.ds(first + self.src_shift, self.rows)
        here = pl.ds(first + self.dst_shift, self.rows)
        return pltpu.make_async_copy(self.src.at[there], self.dst.at[here], self.sems.at[k])

    def start(self):
        for k in range(self.parts):
            self.copy(k).start()

    def wait(self):
        for k in range(self.parts):
            self.copy(k).wait()


def sds(*shape, dtype=F32):
    return jax.ShapeDtypeStruct(shape, dtype)


def head_mask(heads, width):
    lane = lax.broadcasted_iota(jnp.int32, (heads, width), 1)
    row = lax.broadcasted_iota(jnp.int32, (heads, width), 0)
    size = width // heads
    return (lane >= row * size) & (lane < (row + 1) * size)


def eye_mask(n):
    return lax.broadcasted_iota(jnp.int32, (n, n), 0) == lax.broadcasted_iota(jnp.int32, (n, n), 1)


def packed(x):
    rows, block = x.shape
    half, rest = rows // 2, LANES - block
    low = x[half:]
    right = jnp.concatenate([low[: half // 2, rest:], low[half // 2 :, rest:]], axis=1)
    return jnp.concatenate([jnp.concatenate([x[:half], low[:, :rest]], axis=1), right], axis=0)


def unpacked(x, rows, block):
    half, wide = rows // 2, 2 * block - LANES
    top, low = x[:half], x[half:]
    left = top[:, block:]
    lower = [
        jnp.concatenate([left[: half // 2], low[:, :wide]], axis=1),
        jnp.concatenate([left[half // 2 :], low[:, wide:]], axis=1),
    ]
    return jnp.concatenate([top[:, :block]] + lower, axis=0)


def first_kernel(single_ref, cot_ref, wout_ref, out_ref, packed_ref):
    packed_ref[...] = packed(single_ref[...])
    n, _, lanes = out_ref.shape
    rows, block = single_ref.shape
    rest = lanes - block
    half = rows // 2
    single = single_ref[...]
    ch, cl = split(cot_ref[...])
    wh, wl = split(wout_ref[...])
    two = dg(jnp.concatenate([ch, cl], axis=0), wh, NN)
    full = two[:rows] + two[rows:] + dg(ch, wl, NN)
    for k in range(n):
        part = full[:, k * block : (k + 1) * block]
        out_ref[k, :rows, :block] = single
        out_ref[k, :rows, block:] = part[:, :rest]
        out_ref[k, rows:, : block - rest] = part[:half, rest:]
        out_ref[k, rows:, block - rest :] = part[half:, rest:]


def joined_norm(blocks, out_ref, row):
    rows, block = blocks[0].shape
    width = block * len(blocks)
    centre = sum(jnp.sum(b, axis=-1, keepdims=True) for b in blocks) / width
    blocks = [b - centre for b in blocks]
    spread = sum(jnp.sum(b * b, axis=-1, keepdims=True) for b in blocks) / width
    scale = lax.rsqrt(spread + EPS)
    for k, b in enumerate(blocks):
        part = slice(k * block, (k + 1) * block)
        out_ref[row : row + rows, part] = b * scale


def gained(normed, gain_ref):
    tiles, lanes = gain_ref.shape
    parts = [
        split(normed[:, t * lanes : (t + 1) * lanes] * gain_ref[t : t + 1, :]) for t in range(tiles)
    ]
    return jnp.concatenate(
        [jnp.concatenate([p[k] for p in parts], axis=1) for k in range(2)], axis=0
    )


def project(both, weight, copies):
    rows = both.shape[0] // 2
    third = weight.shape[0] // 3
    out = None
    for k, one in enumerate(copies):
        one.wait()
        here = slice(k * third, (k + 1) * third)
        wh, wl = split(weight[here, :])
        two = dg(both[:, here], wh, NN)
        part = two[:rows] + two[rows:] + dg(both[:rows, here], wl, NN)
        out = part if out is None else out + part
    return out


def fetch(src, dst, sems):
    rows = src.shape[0] // 3
    out = []
    for k in range(3):
        here = pl.ds(k * rows, rows)
        one = pltpu.make_async_copy(src.at[here], dst.at[here], sems.at[k])
        one.start()
        out.append(one)
    return out


def back_kernel(recv_ref, back_ref):
    rows, block = back_ref.shape[0] * 4 // 3, back_ref.shape[1] * 3 // 4
    total = recv_ref[0]
    for k in range(1, recv_ref.shape[0]):
        total = total + recv_ref[k]
    rest = total.shape[1] - block
    right = jnp.concatenate([total[rows:, : block - rest], total[rows:, block - rest :]], axis=0)
    total = jnp.concatenate([total[:rows, block:], right], axis=1)
    back_ref[...] = packed(total)


def query_kernel(
    pair_far, wb, pgain, recv, gain, wq_far, wg_far,
    bias_far, rs_far, query_ref, gate_ref,
    x_ref, bias_ref, rs_ref, sems, normed, wq, wg, qsem, gsem,
):
    take, give = bias_streams(pair_far, bias_far, rs_far, x_ref, bias_ref, rs_ref, sems, 1)
    query_copies = fetch(wq_far, wq, qsem)
    gate_copies = fetch(wg_far, wg, gsem)
    bias_rows(take, give, wb.ready(), pgain.ready(), x_ref, bias_ref, rs_ref)
    recv_ref = recv.ready()
    n = recv_ref.shape[0]
    rows, width = query_ref.shape
    joined_norm([recv_ref[k, :rows, : width // n] for k in range(n)], normed, 0)
    both = gained(normed, gain.ready())
    query_ref[...] = project(both, wq, query_copies) * (48 ** -0.5)
    gate_ref[...] = 1.0 / (1.0 + jnp.exp(-project(both, wg, gate_copies)))
    for g in give:
        g.wait()


def centred(x):
    return x - jnp.sum(x, axis=-1, keepdims=True) * (1.0 / x.shape[-1])


def bias_streams(pair_far, bias_far, rs_far, x_ref, bias_ref, rs_ref, sems, part):
    parts = PARTS // 2
    take = Stream(pair_far, x_ref, sems.at[0], parts, part * LARGE)
    take.start()
    return take, [Stream(bias_ref, bias_far, sems.at[1], 1), Stream(rs_ref, rs_far, sems.at[2], 1)]


def bias_rows(take, give, wb_ref, pgain_ref, x_ref, bias_ref, rs_ref):
    chans = x_ref.shape[2]
    heads = bias_ref.shape[1]
    wh, wl = split(wb_ref[...] * pgain_ref[...])
    top = jnp.concatenate([wh, wh], axis=1)
    left = jnp.concatenate([top, jnp.concatenate([wl, jnp.zeros_like(wl)], axis=1)], axis=0)
    ones = jnp.ones((8, 2 * chans), BF16)

    def step(k, carry):
        take.copy(k).wait()
        for j in range(take.rows):
            i = k * take.rows + j
            d = centred(x_ref[i])
            spread = dg(ones, jnp.concatenate(split(d * d), axis=1), NT) * (1.0 / chans)
            rs = lax.rsqrt(spread[0:1] + EPS)
            two = dg(left, jnp.concatenate(split(d), axis=1), NT)
            bias_ref[i] = (two[:heads] + two[heads:]) * rs
            rs_ref[pl.ds(i, 1), :] = rs
        return carry

    lax.fori_loop(0, take.parts, step, 0)
    for g in give:
        g.start()


def pair_kernel(pair_far, wb, pgain, bias_far, rs_far, x_ref, bias_ref, rs_ref, sems):
    take, give = bias_streams(pair_far, bias_far, rs_far, x_ref, bias_ref, rs_ref, sems, 0)
    bias_rows(take, give, wb.ready(), pgain.ready(), x_ref, bias_ref, rs_ref)
    for g in give:
        g.wait()


def halves(heads, width):
    return [
        (slice(g * heads // 2, (g + 1) * heads // 2), slice(g * width // 2, (g + 1) * width // 2))
        for g in range(2)
    ]


def by_head(rows, mask):
    wide = jnp.where(mask, rows[:, None, :], 0.0)
    return split(wide.reshape(-1, rows.shape[1]))


def against(rows, mask, high, low):
    keys = high.shape[0]
    rh, rl = by_head(rows, mask)
    two = dg(rh, jnp.concatenate([high, low], axis=0), NT)
    return two[:, :keys] + two[:, keys:] + dg(rl, high, NT)


def attend_kernel(
    own, far_a, far_b, far_c, gain, wk_far, wv_far, query, bias_a, bias_b, back_four, back_far, gate,
    pay_ref, expo_ref, dprobs_ref, stat_ref,
    normed, wk, wv, dctx, acc, ksem, vsem,
):
    key_copies = fetch(wk_far, wk, ksem)
    for later in (query, bias_a, bias_b):
        later.start()
    value_copies = fetch(wv_far, wv, vsem)
    for later in (back_four, back_far, gate):
        later.start()
    blocks = [piece.ready() for piece in (own, far_a, far_b, far_c)]
    n_sub = blocks[0].shape[0]
    queries, heads, keys = expo_ref.shape
    width = normed.shape[1]
    rows, n_col = queries, pay_ref.shape[0]
    block = width // n_col
    me = lax.axis_index("row")
    col = lax.axis_index("col")

    def token_block(k, core):
        there = place(k, col, core)
        hop = (me // n_sub + 4 - there // n_sub) % 4
        spot = (me % n_sub) ^ (there % n_sub)
        some = [piece[spot] for piece in blocks]
        one = jnp.where(
            hop < 2, jnp.where(hop == 0, some[0], some[1]), jnp.where(hop == 2, some[2], some[3])
        )
        return unpacked(one, rows, block)

    for t in range(keys // rows):
        joined_norm([token_block(k, t) for k in range(n_col)], normed, t * rows)
    both = gained(normed, gain.ready())
    kh, kl = split(project(both, wk, key_copies))
    half = heads // 2
    mask = head_mask(half, width // 2)[None]
    eye = eye_mask(half)[None]

    def lanes(column):
        return jnp.sum(jnp.where(eye, column.reshape(queries, half, 1), 0.0), axis=1)

    parts = []
    query_ref = query.ready()
    bias_refs = [bias_a.ready(), bias_b.ready()]
    for some, part in halves(heads, width):
        bias = jnp.concatenate([b[:, some] for b in bias_refs], axis=0)
        scores = against(query_ref[:, part], mask, kh[:, part], kl[:, part])
        scores = scores + bias.reshape(queries * half, keys)
        top = jnp.max(scores, axis=-1, keepdims=True)
        expo = jnp.exp(scores - top)
        total = jnp.sum(expo, axis=-1, keepdims=True)
        expo_ref[:, some] = expo.reshape(queries, half, keys)
        stat_ref[:, some] = lanes(top)
        lse = lanes(top + jnp.log(total))
        for k in range(n_col):
            pay_ref[k, :, block + some.start : block + some.stop] = lse
        parts.append(expo * (1.0 / total))
    vh, vl = split(project(both, wv, value_copies))
    backs, gate_ref = [back_four.ready(), back_far.ready()], gate.ready()
    n_x = backs[0].shape[0]
    for k in range(n_col):
        part = slice(k * block, (k + 1) * block)
        spot = (col + n_x - k) % n_x
        near = col // n_x == k // n_x
        one = jnp.where(near, backs[0][spot], backs[1][spot])
        dctx[:, part] = unpacked(one, rows, block) * gate_ref[:, part]
    for (some, part), probs in zip(halves(heads, width), parts):
        high, low = vh[:, part], vl[:, part]
        eh, el = split(probs)
        wide = dg(jnp.concatenate([eh, el], axis=1), jnp.concatenate([high, high], axis=0), NN)
        wide = wide + dg(eh, low, NN)
        wide = jnp.where(mask, wide.reshape(queries, half, width // 2), 0.0)
        acc[:, part] = jnp.sum(wide, axis=1)
        dp = against(dctx[:, part], mask, high, low)
        dprobs_ref[:, some] = dp.reshape(queries, half, keys)
        delta = lanes(jnp.sum(probs * dp, axis=-1, keepdims=True))
        for k in range(n_col):
            pay_ref[k, :, block + heads + some.start : block + heads + some.stop] = delta
    for k in range(n_col):
        pay_ref[k, :, :block] = acc[:, k * block : (k + 1) * block]


def moment_kernel(
    x_far, expo_far, dprobs_far, rs_a, rs_b, out_far, x_ref, expo_ref, dprobs_ref, out_ref, sems
):
    heads = expo_ref.shape[1]
    chans = out_ref.shape[2]
    take = [
        Stream(x_far, x_ref, sems.at[0]),
        Stream(expo_far, expo_ref, sems.at[1], 1),
        Stream(dprobs_far, dprobs_ref, sems.at[2], 1),
    ]
    give = Stream(out_ref, out_far, sems.at[3])
    for t in reversed(take):
        t.start()
    for t in take[1:]:
        t.wait()
    cut = PARTS * LARGE // expo_ref.shape[0]

    def step(rs_ref, shift, k, carry):
        take[0].copy(k).wait()
        for j in range(take[0].rows):
            i = k * take[0].rows + j
            e = expo_ref[i] * rs_ref[pl.ds(i - shift, 1), :]
            bh, bl = split(jnp.concatenate([e * dprobs_ref[i], e], axis=0))
            d2 = jnp.concatenate(split(centred(x_ref[i])), axis=1)
            wide = dg(jnp.concatenate([bh, bl], axis=0), d2, NN)
            high = wide[: 2 * heads]
            out_ref[i] = high[:, :chans] + high[:, chans:] + wide[2 * heads :, :chans]
        return carry

    lax.fori_loop(0, cut, functools.partial(step, rs_a.ready(), 0), 0)
    for k in range(cut):
        give.copy(k).start()
    lax.fori_loop(cut, PARTS, functools.partial(step, rs_b.ready(), LARGE), 0)
    for k in range(cut, PARTS):
        give.copy(k).start()
    give.wait()


def join_kernel(recv_ref, stat_ref, moment_ref, pgain_ref, pay_ref, join_ref):
    n, rows, lanes = recv_ref.shape
    heads = moment_ref.shape[1] // 2
    block = lanes - 2 * heads
    size = n * block // heads
    lane = lax.broadcasted_iota(jnp.int32, (heads, block), 1) + lax.axis_index("col") * block
    row = lax.broadcasted_iota(jnp.int32, (heads, block), 0) * size
    sel = jnp.where((lane >= row) & (lane < row + size), 1.0, 0.0)
    lse = [recv_ref[k, :, block : block + heads] for k in range(n)]
    top = functools.reduce(jnp.maximum, lse)
    weight = [jnp.exp(v - top) for v in lse]
    total = sum(weight)
    inv = 1.0 / total
    weight = [w * inv for w in weight]
    delta = sum(w * recv_ref[k, :, block + heads :] for k, w in enumerate(weight))
    fac = jnp.exp(stat_ref[:, :heads] - (top + jnp.log(total)))
    join_ref[:, :heads] = fac
    join_ref[:, heads : 2 * heads] = delta
    context = sum(
        lax.dot_general(w, sel, NN, precision=lax.Precision.HIGHEST, preferred_element_type=F32)
        * recv_ref[k, :, :block]
        for k, w in enumerate(weight)
    )
    eye = eye_mask(heads)[None]

    def column(v):
        return jnp.sum(jnp.where(eye, v[:, None, :], 0.0), axis=-1, keepdims=True)

    part = jnp.sum(
        column(fac) * moment_ref[:, :heads] - column(fac * delta) * moment_ref[:, heads:], axis=0
    ) * pgain_ref[...]
    whole = jnp.concatenate([packed(context), part], axis=0)
    for k in range(n):
        pay_ref[k] = whole


def grad_kernel(
    part, x_far, expo_far, dprobs_far, bias_far, rs, joined, wb, pgain, *refs
):
    if part == 0:
        out_far, x_ref, expo_ref, dprobs_ref, bias_ref, fac_ref, dlt_ref, out_ref, sems = refs
    else:
        _, recv, gate, wout, out_far, att_ref = refs[:6]
        x_ref, expo_ref, dprobs_ref, bias_ref, fac_ref, dlt_ref, out_ref, sems, gated = refs[6:]
    count, keys = out_ref.shape[:2]
    shift = part * LARGE
    parts = PARTS // 2
    take = [
        Stream(x_far, x_ref, sems.at[0], parts, shift),
        Stream(expo_far, expo_ref, sems.at[1], 1, shift),
        Stream(dprobs_far, dprobs_ref, sems.at[2], 1, shift),
        Stream(bias_far, bias_ref, sems.at[3], 1),
    ]
    give = Stream(out_ref, out_far, sems.at[4], parts, shift)
    for t in reversed(take):
        t.start()
    heads = expo_ref.shape[1]
    chans = out_ref.shape[2]
    eye = eye_mask(heads)
    wt = centred(wb.ready()[...] * pgain.ready()[...])
    join_ref = joined.ready()
    rs_ref = rs.ready()
    zero = jnp.zeros_like(wt)
    mean = jnp.full_like(wt, 1.0 / chans)
    wh, wl = split(
        jnp.concatenate(
            [jnp.concatenate([wt, zero], axis=1), jnp.concatenate([zero, mean], axis=1)], axis=0
        )
    )

    def spread(w):
        nil = jnp.zeros_like(w)
        rows = [
            jnp.concatenate([w if m == n else nil for n in range(GROUP)], axis=1)
            for m in range(GROUP)
        ]
        return jnp.concatenate(rows, axis=0)

    weights = jnp.concatenate([spread(wh), spread(wh)], axis=0)
    rest = spread(wl)
    mask = eye[None]

    def columns(first):
        value = join_ref[pl.ds(shift, count), first : first + heads]
        value = jnp.where(mask, value[:, None, :], 0.0).reshape(count * heads, heads)
        high, rest = split(value)
        low, least = split(value - high.astype(F32))
        ones = jnp.ones((3 * heads, keys), BF16)
        return dg(jnp.concatenate([high, low, least], axis=1), ones, NN).reshape(count, heads, keys)

    fac_ref[...] = columns(0)
    dlt_ref[...] = columns(heads)
    for t in take[1:]:
        t.wait()

    def cells(i):
        rs = rs_ref[pl.ds(i, 1), :]
        u = expo_ref[i] * fac_ref[i] * (dprobs_ref[i] - dlt_ref[i]) * rs
        return [u, u * bias_ref[i] * rs]

    def step(k, carry):
        take[0].copy(k).wait()
        for j in range(0, give.rows, GROUP):
            first = k * give.rows + j
            rows = [part for m in range(GROUP) for part in cells(first + m)]
            high, low = split(jnp.concatenate(rows, axis=0).T)
            wide = dg(jnp.concatenate([high, low], axis=1), weights, NN) + dg(high, rest, NN)
            for m in range(GROUP):
                one = wide[:, 2 * chans * m : 2 * chans * (m + 1)]
                i = first + m
                out_ref[i] = one[:, :chans] - centred(x_ref[i]) * one[:, chans:]
        give.copy(k).start()
        return carry

    lax.fori_loop(0, parts, step, 0)
    if part == 1:
        attended_rows(recv.ready(), gate.ready(), wout.ready(), att_ref, gated)
    give.wait()


def share_kernel(recv_ref, pay_ref):
    heads = pay_ref.shape[1]
    rows = recv_ref.shape[1] - heads
    total = recv_ref[0, rows:, :]
    for k in range(1, recv_ref.shape[0]):
        total = total + recv_ref[k, rows:, :]
    for k in range(pay_ref.shape[0]):
        pay_ref[k] = total


def attended_rows(recv_ref, gate_ref, wout_ref, att_ref, gated):
    rows, block = att_ref.shape
    for k in range(recv_ref.shape[0]):
        part = slice(k * block, (k + 1) * block)
        held = recv_ref[k, : rows * block // LANES]
        gated[:, part] = unpacked(held, rows, block) * gate_ref[:, part]
    att_ref[...] = dot3(gated[...], wout_ref[...], NT)


def last_kernel(recv_ref, out_ref):
    total = recv_ref[0]
    for k in range(1, recv_ref.shape[0]):
        total = total + recv_ref[k]
    out_ref[...] = total


def place(col, owner, core):
    high, x = col // 4, col % 4
    y, low = owner // 2, owner % 2
    spot = (y + 6 - x + owner % 4) % 4
    near = lax.select(high == owner // 4, low, 1 - low) if not isinstance(owner, int) else (
        low if high == owner // 4 else 1 - low
    )
    return (spot * 2 + near) * 2 + core


def swap(x, axis):
    return lax.all_to_all(x, axis, 0, 0, tiled=True)


def local(
    single, pair, single_gain, pair_gain, w_query, w_key, w_value, w_gate, w_bias, w_out, cotangent
):
    n_row, n_col = lax.axis_size("row"), lax.axis_size("col")
    queries, keys, chans = pair.shape
    heads = w_bias.shape[1]
    width = single_gain.shape[0]
    block = single.shape[1]
    per = n_row // n_col
    gain = single_gain.reshape(-1, chans)
    pgain = pair_gain[None]
    wb = w_bias.T
    wout = w_out.T
    dma = pltpu.SemaphoreType.DMA
    shape_e = sds(queries, heads, keys)

    def mem(shape):
        return pltpu.VMEM(shape.shape, shape.dtype)

    perm = [
        (r * n_col + c, place(c, r // per, r % per) * n_col + r // per)
        for r in range(n_row)
        for c in range(n_col)
    ]
    pay1, packed_single = call(
        first_kernel,
        (sds(n_col, queries + queries // 2, chans), sds(queries * block // LANES, LANES)),
        2 * queries * width * block * 3,
        (single, cotangent, wout),
    )
    moved = lax.ppermute(packed_single, ("row", "col"), perm)
    recv1 = swap(pay1, "col")
    shape_x = sds(queries, keys, chans)
    counts = (LARGE, queries - LARGE)
    parts_e = [sds(n, heads, keys) for n in counts]
    parts_rs = [sds(n, keys) for n in counts]
    parts_x = [sds(n, keys, chans) for n in counts]
    held = [
        [mem(x), mem(e), mem(rs), dma((3, PARTS // 2))]
        for x, e, rs in zip(parts_x, parts_e, parts_rs)
    ]
    bias_a, rs_a = call(
        pair_kernel,
        (parts_e[0], parts_rs[0]),
        queries * keys * chans * 200,
        (pair, wb, pgain),
        held[0],
        (0, 1, 1),
        (1, 1),
    )
    moved, rs_a = lax.optimization_barrier((moved, rs_a))

    def along(x, target):
        return lax.ppermute(x, "row", [(r, target(r)) for r in range(n_row)])

    pair_of = jnp.stack([moved, along(moved, lambda r: r ^ 1)])
    back_pay = call(back_kernel, sds(queries * block // LANES, LANES), queries * width, (recv1,), vmem=4 * MIB)
    four = jnp.concatenate([pair_of, along(pair_of, lambda r: r ^ 2)])
    n_x = 4

    def around(x, k):
        return lax.ppermute(x, "col", [(c, c - c % n_x + (c + k) % n_x) for c in range(n_col)])

    back_four = jnp.stack([back_pay] + [around(back_pay, k) for k in range(1, n_x)])
    back_far = lax.ppermute(back_four, "col", [(c, (c + n_x) % n_col) for c in range(n_col)])
    ring = [along(four, lambda r: (r + 4 * k) % n_row) for k in range(1, 4)]
    recv1, four = lax.optimization_barrier((recv1, four))
    square = pltpu.VMEM((width, width), F32)
    bias_b, rs_b, query, gate = call(
        query_kernel,
        (
            parts_e[1],
            parts_rs[1],
            sds(queries, width),
            sds(queries, width),
        ),
        queries * keys * chans * 200 + queries * width * width * 12,
        (pair, wb, pgain, recv1, gain, w_query, w_gate),
        held[1] + [pltpu.VMEM((queries, width), F32), square, square, dma((3,)), dma((3,))],
        (0, 1, 1, 1, 1, 0, 0),
        (1, 1, 0, 0),
    )
    pay4, expo, dprobs, stat = call(
        attend_kernel,
        (sds(n_col, queries, chans), shape_e, shape_e, sds(queries, chans)),
        keys * width * width * 12,
        (four, *ring, gain, w_key, w_value, query, bias_a, bias_b, back_four, back_far, gate),
        [
            pltpu.VMEM((keys, width), F32),
            square,
            square,
            pltpu.VMEM((queries, width), F32),
            pltpu.VMEM((queries, width), F32),
            dma((3,)),
            dma((3,)),
        ],
        (1, 1, 1, 1, 1, 0, 0, 2, 2, 2, 2, 2, 2),
    )
    recv4 = swap(pay4, "col")
    shape_m = sds(queries, 2 * heads, chans)
    moment = call(
        moment_kernel,
        shape_m,
        queries * keys * chans * heads * 12,
        (pair, expo, dprobs, rs_a, rs_b),
        [mem(shape_x), mem(shape_e), mem(shape_e), mem(shape_m), dma((4, PARTS))],
        (0, 0, 0, 1, 1),
        (1,),
    )
    pay5, joined = call(
        join_kernel,
        (sds(n_col, queries * block // LANES + heads, chans), sds(queries, chans)),
        queries * heads * chans * 8,
        (recv4, stat, moment, pgain),
    )
    recv5 = swap(pay5, "col")
    cost = queries * keys * chans * 200
    held = [
        [mem(x)] + 5 * [mem(e)] + [mem(x), dma((5, PARTS // 2))] for x, e in zip(parts_x, parts_e)
    ]
    place_of = (0, 0, 0, 0, 1, 1, 1, 1)
    first = call(
        functools.partial(grad_kernel, 0),
        shape_x,
        cost,
        (pair, expo, dprobs, bias_a, rs_a, joined, wb, pgain),
        held[0],
        place_of,
        (1,),
    )
    recv5, first = lax.optimization_barrier((recv5, first))
    pay6 = call(
        share_kernel, sds(n_row, heads, chans), queries * width, (recv5,), vmem=4 * MIB
    )
    recv6 = swap(pay6, "row")
    pair_grad, attended = call(
        functools.partial(grad_kernel, 1),
        (shape_x, sds(queries, block)),
        cost,
        (pair, expo, dprobs, bias_b, rs_b, joined, wb, pgain, first, recv5, gate, wout),
        held[1] + [pltpu.VMEM((queries, width), F32)],
        place_of + (0, 1, 1, 1),
        (1, 0),
        {8: 0},
    )
    recv6, pair_grad, attended = lax.optimization_barrier((recv6, pair_grad, attended))
    bias_grad = call(last_kernel, sds(heads, chans), chans * heads, (recv6,), vmem=4 * MIB)
    return attended, pair_grad, bias_grad.T


def solution(mesh):
    placed = (
        P("row", "col"),
        P("row", "col", None),
        P(),
        P(),
        P(),
        P(),
        P(),
        P(),
        P(),
        P(None, "col"),
        P("row", "col"),
    )
    return jax.shard_map(
        local,
        mesh=mesh,
        in_specs=placed,
        out_specs=(P("row", "col"), P("row", "col", None), P()),
        check_vma=False,
    )
```
